128 devices in a mesh: shard: 16 (over y, x), ctx: 4 (over z_lo, core), tp: 2 (over z_hi).
Axes of the slice: x: 4, y: 4, z: 4 (z_hi: 2, z_lo: 2; z = z_hi * 2 + z_lo), core: 2. Of those that a mesh axis runs over, the one named last changes fastest.
Arguments:
- tokens: float32 [20480, 960], P(('shard', 'ctx', 'tp')), may hold values from -6 to 6
- segment_ids: int32 [20480], P(('shard', 'ctx', 'tp')), may hold values from 0 to 4, as said below
- positions: int32 [20480], P(('shard', 'ctx', 'tp')), may hold values from 0 to 1023, as said below
- cotangent: float32 [20480, 960], P(('shard', 'ctx', 'tp')), may hold values from -6 to 6
- attn_gain: bfloat16 [2, 960], P(None, 'shard'), may hold values from 0.5 to 1.5
- w_query: bfloat16 [2, 960, 960], P(None, 'shard'), may hold values from -6 to 6
- w_key: bfloat16 [2, 960, 320], P(None, 'shard'), may hold values from -6 to 6
- w_value: bfloat16 [2, 960, 320], P(None, 'shard'), may hold values from -0.1875 to 0.1875
- w_out: bfloat16 [2, 960, 960], P(None, 'shard'), may hold values from -3 to 3
- ffn_gain: bfloat16 [2, 960], P(None, 'shard'), may hold values from 0.5 to 1.5
- w_gate: bfloat16 [2, 960, 2560], P(None, 'shard', 'tp'), may hold values from -0.1875 to 0.1875
- w_up: bfloat16 [2, 960, 2560], P(None, 'shard', 'tp'), may hold values from -0.1875 to 0.1875
- w_down: bfloat16 [2, 960, 2560], P(None, 'shard', 'tp'), may hold values from -0.125 to 0.125
Outputs:
- block_out: float32 [20480, 960], P(('shard', 'ctx', 'tp'))
- input_grad: float32 [20480, 960], P(('shard', 'ctx', 'tp'))
- grad_attn_gain: float32 [2, 960], P(None, 'shard')
- grad_w_query: float32 [2, 960, 960], P(None, 'shard')
- grad_w_key: float32 [2, 960, 320], P(None, 'shard')
- grad_w_value: float32 [2, 960, 320], P(None, 'shard')
- grad_w_out: float32 [2, 960, 960], P(None, 'shard')
- grad_ffn_gain: float32 [2, 960], P(None, 'shard')
- grad_w_gate: float32 [2, 960, 2560], P(None, 'shard', 'tp')
- grad_w_up: float32 [2, 960, 2560], P(None, 'shard', 'tp')
- grad_w_down: float32 [2, 960, 2560], P(None, 'shard', 'tp')
The draws below stay inside these ranges and needn't reach their ends.
Inputs may be any that keep to these rules, and one draw needn't show every extreme that they name: `segment_ids`: within each block of 1280 consecutive tokens (one index of shard), ids never fall and a sequence's tokens are consecutive; exactly one sequence has 1024 tokens and every other has fewer. positions[t] counts the earlier tokens of t's sequence in its block.
All inputs are finite; a program needn't handle non-finite values.
Results may differ from the reference program's by a relative error of at most 0.023.
Values may be sent and summed in bfloat16 or wider, within the bound.
No kernel may reach another device: no remote copies, remote signals or barrier semaphores. Data moves between devices by JAX's collectives and lax.ppermute only.
A program may use at most 256 MiB of HBM per device.

```python
import jax
import jax.numpy as jnp
from jax import lax

D = 960
HEADS = 15
KV_HEADS = 5
HEAD = 64
FF = 2560
LAYERS = 2
QW = 960
KVW = 320
GROUP = 1280
LONGEST = 1024
TOKENS = 20480
N_SHARD = 16


def layout_draw(key):
    base_key = jax.random.fold_in(key, 7)
    group_keys = jax.random.split(base_key, N_SHARD)

    def one_group(group_key):
        key_one, key_two, key_three = jax.random.split(group_key, 3)
        spare_room = GROUP - LONGEST
        long_start = jax.random.randint(key_one, (), 0, spare_room + 1)
        early_cut = jax.random.randint(key_two, (), 0, long_start + 1)
        late_cut = jax.random.randint(key_three, (), long_start + LONGEST, GROUP + 1)
        slot_index = jnp.arange(GROUP, dtype=jnp.int32)
        segment = (slot_index >= early_cut).astype(jnp.int32) + (slot_index >= long_start).astype(jnp.int32) + (slot_index >= long_start + LONGEST).astype(jnp.int32) + (slot_index >= late_cut).astype(jnp.int32)
        seg_begin = jnp.where(segment >= 1, early_cut, 0)
        seg_begin = jnp.where(segment >= 2, long_start, seg_begin)
        seg_begin = jnp.where(segment >= 3, long_start + LONGEST, seg_begin)
        seg_begin = jnp.where(segment >= 4, late_cut, seg_begin)
        return (segment.astype(jnp.int32), (slot_index - seg_begin).astype(jnp.int32))
    segments, places = jax.vmap(one_group)(group_keys)
    return (segments.reshape(-1), places.reshape(-1))


def draw_segment_ids(key, part):
    return layout_draw(key)[0]


def draw_positions(key, part):
    return layout_draw(key)[1]


def query_key_draw(key):
    base_key = jax.random.fold_in(key, 11)
    query_seed, key_seed = jax.random.split(base_key)
    query_weight = jnp.clip(jax.random.normal(query_seed, (LAYERS, D, HEADS * HEAD), jnp.float32), -6.0, 6.0) * D ** (-0.5)
    key_weight = jnp.clip(jax.random.normal(key_seed, (LAYERS, D, KV_HEADS * HEAD), jnp.float32), -6.0, 6.0) * D ** (-0.5)
    return (query_weight, key_weight)


def draw_w_query(key, part):
    return query_key_draw(key)[0].astype(jnp.bfloat16)


def draw_w_key(key, part):
    return query_key_draw(key)[1].astype(jnp.bfloat16)


def steps_of(own_key, dims, shards, smallest, largest):
    def one(axis_at, blocks):
        heights = jax.random.uniform(jax.random.fold_in(jax.random.fold_in(own_key, 6), axis_at), (blocks,), jnp.float32, smallest / len(shards), largest / len(shards))
        return jnp.repeat(jnp.exp(heights), dims[axis_at] // blocks).reshape((-1,) + (1,) * (len(dims) - axis_at - 1))

    factor_of = one(*shards[0])
    for cut in shards[1:]:
        factor_of = factor_of * one(*cut)
    return factor_of


def gaussian(stream_key, shape, deviation, limit, cuts=(), kind=jnp.bfloat16):
    loudness = steps_of(stream_key, shape, cuts, -0.22, 0.18) if cuts else 1.0
    drawn = jax.random.normal(stream_key, shape, jnp.float32) * deviation * loudness
    return jnp.minimum(jnp.maximum(drawn, -limit), limit).astype(kind)


def setup_inputs(seed: int = 0) -> dict:
    key_list = jax.random.split(jax.random.key(seed), 14)
    tokens = gaussian(key_list[0], (TOKENS, D), 1.0, 6.0, ((0, 128),), jnp.float32)
    segment_ids = draw_segment_ids(jax.random.fold_in(key_list[13], 71), 0)
    positions = draw_positions(jax.random.fold_in(key_list[13], 71), 0)
    cotangent = gaussian(key_list[3], (TOKENS, D), 1.0, 6.0, ((0, 128),), jnp.float32)
    attn_gain = jnp.clip(1.0 + 0.1 * jax.random.normal(key_list[4], (LAYERS, D), jnp.float32), 0.5, 1.5).astype(jnp.bfloat16)
    w_query = draw_w_query(jax.random.fold_in(key_list[13], 71), 0)
    w_key = draw_w_key(jax.random.fold_in(key_list[13], 71), 0)
    w_value = gaussian(key_list[7], (LAYERS, D, KVW), D ** -0.5, 0.1875, ((1, 16),))
    w_out = gaussian(key_list[8], (LAYERS, D, QW), 4 ** -0.5, 3.0, ((1, 16),))
    ffn_gain = jnp.clip(1.0 + 0.1 * jax.random.normal(key_list[9], (LAYERS, D), jnp.float32), 0.5, 1.5).astype(jnp.bfloat16)
    w_gate = gaussian(key_list[10], (LAYERS, D, FF), D ** -0.5, 0.1875, ((1, 16), (2, 2)))
    w_up = gaussian(key_list[11], (LAYERS, D, FF), D ** -0.5, 0.1875, ((1, 16), (2, 2)))
    w_down = gaussian(key_list[12], (LAYERS, D, FF), FF ** -0.5, 0.125, ((1, 16), (2, 2)))
    return dict(tokens=tokens, segment_ids=segment_ids, positions=positions, cotangent=cotangent, attn_gain=attn_gain, w_query=w_query, w_key=w_key, w_value=w_value, w_out=w_out, ffn_gain=ffn_gain, w_gate=w_gate, w_up=w_up, w_down=w_down)


EPSILON = 1e-05
THETA = 100000.0
MASKED = -1e+30

def product(left, right):
    return jnp.dot(left, right, preferred_element_type=jnp.float32)

def head_einsum(form, left, right):
    return jnp.einsum(form, left.astype(jnp.float32), right.astype(jnp.float32))

def rope_tables(positions):
    half_head = HEAD // 2
    freqs = THETA ** (-2.0 * jnp.arange(half_head, dtype=jnp.float32) / HEAD)
    angles = positions.astype(jnp.float32)[:, None] * freqs[None, :]
    return (jnp.cos(angles), jnp.sin(angles))

def rotate(values, cosine, sine, direction):
    row_count = values.shape[0]
    split_view = values.reshape(row_count, -1, 2, HEAD // 2)
    first_half = split_view[:, :, 0]
    second_half = split_view[:, :, 1]
    cos_rows = cosine[:, None, :]
    sin_rows = direction * sine[:, None, :]
    turned = jnp.stack([first_half * cos_rows - second_half * sin_rows, second_half * cos_rows + first_half * sin_rows], axis=2)
    return turned.reshape(row_count, -1)

def rms_forward(values, gain):
    scale = lax.rsqrt(lax.optimization_barrier(jnp.mean(values * values, axis=-1, keepdims=True)) + EPSILON)
    return (values * scale * gain.astype(jnp.float32), scale)

def rms_backward(values, scale, gain, grad_normed):
    weighted = grad_normed * gain.astype(jnp.float32)
    grad_values = scale * weighted - values * (scale * scale * scale) * lax.optimization_barrier(jnp.mean(weighted * values, axis=-1, keepdims=True))
    grad_gain = lax.optimization_barrier(jnp.sum(grad_normed * values * scale, axis=0))
    return (grad_values, grad_gain)

def scores_of(query, keys, visible):
    query_heads = query.reshape(query.shape[0], KV_HEADS, HEADS // KV_HEADS, HEAD)
    key_heads = keys.reshape(keys.shape[0], KV_HEADS, HEAD)
    raw = head_einsum('tghd,sgd->ghts', query_heads, key_heads) * HEAD ** (-0.5)
    return jnp.where(visible[None, None], raw, MASKED)

def group_pass(params, tokens, cotangent, segments, positions):
    cosine, sine = rope_tables(positions)
    visible = (segments[:, None] == segments[None, :]) & (positions[None, :] <= positions[:, None])
    row_count = tokens.shape[0]
    stream = tokens
    saved = []
    for layer in range(LAYERS):
        gain_one, query_weight, key_weight, value_weight, out_weight, gain_two, gate_weight, up_weight, down_weight = tuple((param[layer] for param in params))
        normed_one, scale_one = rms_forward(stream, gain_one)
        normed_one = normed_one.astype(jnp.bfloat16)
        query = rotate(product(normed_one, query_weight), cosine, sine, 1.0).astype(jnp.bfloat16)
        key_rows = rotate(product(normed_one, key_weight), cosine, sine, 1.0).astype(jnp.bfloat16)
        value_rows = product(normed_one, value_weight).astype(jnp.bfloat16)
        scores = scores_of(query, key_rows, visible)
        top = lax.optimization_barrier(jnp.max(scores, axis=-1, keepdims=True))
        log_total = top + jnp.log(lax.optimization_barrier(jnp.sum(jnp.exp(scores - top), axis=-1, keepdims=True)))
        probs = jnp.exp(scores - log_total).astype(jnp.bfloat16)
        attended = head_einsum('ghts,sgd->tghd', probs, value_rows.reshape(row_count, KV_HEADS, HEAD)).reshape(row_count, -1).astype(jnp.bfloat16)
        mixed = stream + product(attended, out_weight.T)
        normed_two, scale_two = rms_forward(mixed, gain_two)
        normed_two = normed_two.astype(jnp.bfloat16)
        gate = product(normed_two, gate_weight)
        up_value = product(normed_two, up_weight)
        sigma = jax.nn.sigmoid(gate)
        swish = gate * sigma
        hidden = (swish * up_value).astype(jnp.bfloat16)
        saved.append((stream, scale_one, normed_one, query, key_rows, value_rows, log_total, attended, mixed, scale_two, normed_two, gate, up_value, sigma, swish, hidden))
        stream = mixed + product(hidden, down_weight.T)
    block_out = stream
    grad_stream = cotangent
    layer_grads = [None] * LAYERS
    for layer in reversed(range(LAYERS)):
        gain_one, query_weight, key_weight, value_weight, out_weight, gain_two, gate_weight, up_weight, down_weight = tuple((param[layer] for param in params))
        layer_input, scale_one, normed_one, query, key_rows, value_rows, log_total, attended, mixed, scale_two, normed_two, gate, up_value, sigma, swish, hidden = saved[layer]
        grad_out_b = grad_stream.astype(jnp.bfloat16)
        grad_hidden = product(grad_out_b, down_weight)
        grad_down = product(grad_out_b.T, hidden)
        grad_up_in = (grad_hidden * swish).astype(jnp.bfloat16)
        grad_gate_in = (grad_hidden * up_value * sigma * (1.0 + gate * (1.0 - sigma))).astype(jnp.bfloat16)
        grad_gate = product(normed_two.T, grad_gate_in)
        grad_up = product(normed_two.T, grad_up_in)
        grad_normed_two = product(grad_gate_in, gate_weight.T) + product(grad_up_in, up_weight.T)
        grad_mixed_norm, grad_gain_two = rms_backward(mixed, scale_two, gain_two, grad_normed_two)
        grad_mixed = grad_stream + grad_mixed_norm
        grad_mixed_b = grad_mixed.astype(jnp.bfloat16)
        grad_attended = product(grad_mixed_b, out_weight)
        grad_out_weight = product(grad_mixed_b.T, attended)
        grad_attended_b = grad_attended.astype(jnp.bfloat16)
        scores = scores_of(query, key_rows, visible)
        probs_exact = jnp.exp(scores - log_total)
        probs = probs_exact.astype(jnp.bfloat16)
        attended_heads = grad_attended_b.reshape(row_count, KV_HEADS, HEADS // KV_HEADS, HEAD)
        query_heads = query.reshape(row_count, KV_HEADS, HEADS // KV_HEADS, HEAD)
        grad_probs = head_einsum('tghd,sgd->ghts', attended_heads, value_rows.reshape(row_count, KV_HEADS, HEAD))
        delta = lax.optimization_barrier(jnp.sum(probs_exact * grad_probs, axis=-1, keepdims=True))
        grad_scores = (probs_exact * (grad_probs - delta) * HEAD ** (-0.5)).astype(jnp.bfloat16)
        grad_query = head_einsum('ghts,sgd->tghd', grad_scores, key_rows.reshape(row_count, KV_HEADS, HEAD)).reshape(row_count, -1)
        grad_key = head_einsum('ghts,tghd->sgd', grad_scores, query_heads).reshape(row_count, -1)
        grad_value = head_einsum('ghts,tghd->sgd', probs, attended_heads).reshape(row_count, -1)
        grad_query_b = rotate(grad_query, cosine, sine, -1.0).astype(jnp.bfloat16)
        grad_key_b = rotate(grad_key, cosine, sine, -1.0).astype(jnp.bfloat16)
        grad_value_b = grad_value.astype(jnp.bfloat16)
        grad_query_weight = product(normed_one.T, grad_query_b)
        grad_key_weight = product(normed_one.T, grad_key_b)
        grad_value_weight = product(normed_one.T, grad_value_b)
        grad_normed_one = product(grad_query_b, query_weight.T) + product(grad_key_b, key_weight.T) + product(grad_value_b, value_weight.T)
        grad_input_norm, grad_gain_one = rms_backward(layer_input, scale_one, gain_one, grad_normed_one)
        grad_stream = grad_mixed + grad_input_norm
        layer_grads[layer] = (grad_gain_one, grad_query_weight, grad_key_weight, grad_value_weight, grad_out_weight, grad_gain_two, grad_gate, grad_up, grad_down)
    stacked = tuple((jnp.stack([layer_grads[layer][index] for layer in range(LAYERS)]) for index in range(9)))
    return (block_out, grad_stream, stacked)

def reference(tokens, segment_ids, positions, cotangent, attn_gain, w_query, w_key, w_value, w_out, ffn_gain, w_gate, w_up, w_down):
    params = (attn_gain, w_query, w_key, w_value, w_out, ffn_gain, w_gate, w_up, w_down)

    def step(carry, inputs):
        group_tokens, group_cotangent, group_segments, group_positions = inputs
        block_part, input_part, grads = group_pass(params, group_tokens, group_cotangent, group_segments, group_positions)
        return (tuple((total + added for total, added in zip(carry, grads))), (block_part, input_part))
    start_grads = tuple((jnp.zeros(param.shape, jnp.float32) for param in params))
    grouped = (tokens.reshape(N_SHARD, GROUP, D), cotangent.reshape(N_SHARD, GROUP, D), segment_ids.reshape(N_SHARD, GROUP), positions.reshape(N_SHARD, GROUP))
    totals, outputs = lax.scan(step, start_grads, grouped)
    block_out = outputs[0].reshape(TOKENS, D)
    input_grad = outputs[1].reshape(TOKENS, D)
    return (block_out, input_grad, totals[0], totals[1], totals[2], totals[3], totals[4], totals[5], totals[6], totals[7], totals[8])
```

```python
import jax
import jax.numpy as jnp
from jax import lax
from jax.sharding import Mesh, PartitionSpec as P

D = 960
HEADS = 15
KV_HEADS = 5
HEAD = 64
QW = HEADS * HEAD
KVW = KV_HEADS * HEAD

EPSILON = 1e-05
THETA = 100000.0
MASKED = -1e30

Y, X, ZL, CORE, TP = 4, 4, 2, 2, 2
XY = ("y", "x")
PER = D // (Y * X)
PAD = 64
DP = PAD * Y * X
QKV_HALF = (QW + 2 * KVW) // 2
QKV_PAD = 896
OUT_HALF = QW // 2
OUT_PAD = 512
ATT = QKV_PAD + OUT_PAD
BF = jnp.bfloat16
F32 = jnp.float32


def product(left, right):
    return jnp.dot(left, right, preferred_element_type=F32)


def by_rows(left, right):
    return lax.dot_general(left, right, (((0,), (0,)), ((), ())), preferred_element_type=F32)


def by_columns(left, right):
    return lax.dot_general(left, right, (((1,), (1,)), ((), ())), preferred_element_type=F32)


def ring(size, step):
    return [(i, (i + step) % size) for i in range(size)]


def z_ring(step):
    pairs = []
    for low in range(ZL):
        for high in range(TP):
            there = (high * ZL + low + step) % (ZL * TP)
            pairs.append((low * TP + high, (there % ZL) * TP + there // ZL))
    return pairs


def swap(values, axis):
    return lax.ppermute(values, axis, [(0, 1), (1, 0)])


def z_send(values, step):
    return lax.ppermute(values, ("zl", "tp"), z_ring(step))


STEPS = (2, 1, 3)


def gather_group(values):
    mine = jnp.concatenate([values] + [z_send(values, step) for step in STEPS], axis=0)
    return jnp.concatenate([mine, swap(mine, "core")], axis=0)


def scatter_group(terms):
    half = terms.shape[0] // 2
    rows = half // 4
    total = terms[:half].astype(F32) + swap(terms[half:].astype(BF), "core").astype(F32)
    out = total[:rows]
    for at, step in enumerate(STEPS):
        block = total[(at + 1) * rows : (at + 2) * rows].astype(BF)
        out = out + z_send(block, -step).astype(F32)
    return out


def line_gather(values, axis):
    at = lax.axis_index(axis)
    out = jnp.zeros((4,) + values.shape, values.dtype)
    out = lax.dynamic_update_index_in_dim(out, values, at, 0)
    for step in STEPS:
        got = lax.ppermute(values, axis, ring(4, step))
        out = lax.dynamic_update_index_in_dim(out, got, (at - step) % 4, 0)
    return out


def plane_gather(values, cut):
    first = line_gather(line_gather(values[:, :cut], "x"), "y")
    second = line_gather(line_gather(values[:, cut:], "y"), "x")
    first = first.reshape(DP, -1)
    second = jnp.swapaxes(second, 0, 1).reshape(DP, -1)
    return first, second


def line_scatter(values, axis):
    at = lax.axis_index(axis)
    out = lax.dynamic_index_in_dim(values, at, 0, False).astype(F32)
    for step in STEPS:
        block = lax.dynamic_index_in_dim(values, (at + step) % 4, 0, False)
        out = out + lax.ppermute(block, axis, ring(4, step)).astype(F32)
    return out


def plane_scatter(values, cut):
    view = values.reshape(Y, X, PAD, values.shape[1])
    first = line_scatter(jnp.swapaxes(view[..., :cut], 0, 1), "x").astype(BF)
    second = line_scatter(view[..., cut:], "y").astype(BF)
    first = line_scatter(first, "y")
    second = line_scatter(second, "x")
    return jnp.concatenate([first, second], axis=1)


def reduce_grads(keep, give, cut, over_tp):
    total = (keep.astype(F32) + swap(give.astype(BF), "core").astype(F32)).astype(BF)
    total = plane_scatter(total, cut).astype(BF)
    total = total.astype(F32) + swap(total, "zl").astype(F32)
    total = total.astype(BF)
    return total


def finish(total, tp_width):
    part = total[:, :tp_width]
    part = (part.astype(F32) + swap(part, "tp").astype(F32)).astype(BF)
    if tp_width < total.shape[1]:
        part = jnp.concatenate([part, total[:, tp_width:]], axis=1)
    return part, swap(part, "core")


def rope_tables(positions):
    half_head = HEAD // 2
    freqs = THETA ** (-2.0 * jnp.arange(half_head, dtype=F32) / HEAD)
    angles = positions.astype(F32)[:, None] * freqs[None, :]
    return (jnp.cos(angles), jnp.sin(angles))


def rotate(values, cosine, sine, direction):
    row_count = values.shape[0]
    split_view = values.reshape(row_count, -1, 2, HEAD // 2)
    first_half = split_view[:, :, 0]
    second_half = split_view[:, :, 1]
    cos_rows = cosine[:, None, :]
    sin_rows = direction * sine[:, None, :]
    turned = jnp.stack(
        [
            first_half * cos_rows - second_half * sin_rows,
            second_half * cos_rows + first_half * sin_rows,
        ],
        axis=2,
    )
    return turned.reshape(row_count, -1)


def rms_forward(values, gain):
    mean = jnp.sum(values * values, axis=-1, keepdims=True) * (1.0 / D)
    scale = lax.rsqrt(mean + EPSILON)
    return (values * scale * gain, scale)


def rms_backward(values, scale, gain, grad_normed):
    weighted = grad_normed * gain
    mean = jnp.sum(weighted * values, axis=-1, keepdims=True) * (1.0 / D)
    grad_values = scale * weighted - values * (scale * scale * scale) * mean
    gain_terms = (grad_normed * values * scale).astype(BF)
    ones = jnp.ones((values.shape[0], OUT_PAD - OUT_HALF), BF)
    return (grad_values, by_rows(gain_terms, ones))


def head_rows(matrix, group, row_count):
    view = matrix.reshape(row_count, KV_HEADS, HEADS // KV_HEADS, HEAD)[:, group]
    return jnp.transpose(view, (1, 0, 2)).reshape(-1, HEAD)


def head_back(block, row_count):
    return jnp.transpose(block.reshape(HEADS // KV_HEADS, row_count, HEAD), (1, 0, 2)).reshape(
        row_count, -1
    )


def masked_scores(query_block, key_block, visible):
    raw = by_columns(query_block, key_block) * HEAD ** (-0.5)
    shaped = raw.reshape(HEADS // KV_HEADS, visible.shape[0], -1)
    return jnp.where(visible[None], shaped, MASKED).reshape(raw.shape)


def attention(query, key_all, value_all, visible):
    row_count = query.shape[0]
    parts = []
    log_totals = []
    for group in range(KV_HEADS):
        query_block = head_rows(query, group, row_count)
        key_block = key_all[:, group * HEAD : (group + 1) * HEAD]
        value_block = value_all[:, group * HEAD : (group + 1) * HEAD]
        scores = masked_scores(query_block, key_block, visible)
        top = jnp.max(scores, axis=-1, keepdims=True)
        log_total = top + jnp.log(jnp.sum(jnp.exp(scores - top), axis=-1, keepdims=True))
        probs = jnp.exp(scores - log_total).astype(BF)
        parts.append(head_back(product(probs, value_block), row_count))
        log_totals.append(log_total)
    return jnp.concatenate(parts, axis=1).astype(BF), log_totals


def attention_back(query, key_all, value_all, visible, log_totals, grad_attended_b):
    row_count = query.shape[0]
    query_parts, key_parts, value_parts = [], [], []
    for group in range(KV_HEADS):
        query_block = head_rows(query, group, row_count)
        grad_block = head_rows(grad_attended_b, group, row_count)
        key_block = key_all[:, group * HEAD : (group + 1) * HEAD]
        value_block = value_all[:, group * HEAD : (group + 1) * HEAD]
        scores = masked_scores(query_block, key_block, visible)
        probs_exact = jnp.exp(scores - log_totals[group])
        probs = probs_exact.astype(BF)
        grad_probs = by_columns(grad_block, value_block)
        delta = jnp.sum(probs_exact * grad_probs, axis=-1, keepdims=True)
        grad_scores = (probs_exact * (grad_probs - delta) * HEAD ** (-0.5)).astype(BF)
        query_parts.append(head_back(product(grad_scores, key_block), row_count))
        key_parts.append(by_rows(grad_scores, query_block))
        value_parts.append(by_rows(probs, grad_block))
    return (
        jnp.concatenate(query_parts, axis=1),
        jnp.concatenate(key_parts + value_parts, axis=1).astype(BF),
    )


def pad_features(values):
    rows = values.shape[0]
    view = values.reshape(rows, Y * X, PER)
    return jnp.pad(view, ((0, 0), (0, 0), (0, PAD - PER))).reshape(rows, DP)


def cut_features(values):
    rows = values.shape[0]
    return values.reshape(rows, Y * X, PAD)[:, :, :PER].reshape(rows, D)


def shards(
    tokens,
    segment_ids,
    positions,
    cotangent,
    attn_gain,
    w_query,
    w_key,
    w_value,
    w_out,
    ffn_gain,
    w_gate,
    w_up,
    w_down,
):
    layers = attn_gain.shape[0]
    rows = tokens.shape[0]
    hid = w_gate.shape[2] // 2
    first_core = lax.axis_index("core") == 0

    def pick(low, high):
        return jnp.where(first_core, low, high), jnp.where(first_core, high, low)

    def halves(whole, width):
        return pick(whole[..., :width], whole[..., width:])

    def join(mine, other):
        low, high = pick(mine, other)
        return jnp.concatenate([low, high], axis=-1)

    def tall(values):
        return jnp.pad(values, ((0, PAD - PER), (0, 0)))

    gain_columns = jnp.stack(
        [attn_gain[layer] for layer in range(layers)] + [ffn_gain[layer] for layer in range(layers)],
        axis=1,
    )
    gain_columns = jnp.pad(gain_columns, ((0, 0), (0, OUT_PAD - OUT_HALF - 2 * layers)))
    packs = []
    for layer in range(layers):
        qkv = jnp.concatenate([w_query[layer], w_key[layer], w_value[layer]], axis=1)
        qkv_mine = jnp.pad(halves(qkv, QKV_HALF)[0], ((0, 0), (0, QKV_PAD - QKV_HALF)))
        out_mine = halves(w_out[layer], OUT_HALF)[0]
        packs.append(jnp.concatenate([qkv_mine, out_mine, gain_columns], axis=1))
        packs.append(
            jnp.concatenate(
                [halves(w[layer], hid)[0] for w in (w_gate, w_up, w_down)], axis=1
            )
        )
    packs = [tall(pack) for pack in packs]
    cut = 768
    early = plane_gather(packs[0], cut)
    early_other = tuple(swap(part, "core") for part in early)
    rest = lax.all_gather(jnp.concatenate(packs[1:], axis=1), XY, axis=0, tiled=True)
    rest_other = swap(rest, "core")

    def early_weights(parts):
        left, right = parts
        out = right[:, QKV_PAD - cut :]
        return jnp.concatenate([left, right[:, : QKV_PAD - cut]], axis=1), out

    def att_weights(whole, base):
        return whole[:, base : base + QKV_PAD], whole[:, base + QKV_PAD : base + ATT]

    def ffn_weights(whole, base):
        return whole[:, base : base + 2 * hid], whole[:, base + 2 * hid : base + 3 * hid]

    att_mine = [early_weights(early), att_weights(rest, 3 * hid)]
    att_other = [early_weights(early_other), att_weights(rest_other, 3 * hid)]
    ffn_mine = [ffn_weights(rest, 0), ffn_weights(rest, 3 * hid + ATT)]
    ffn_other = [ffn_weights(rest_other, 0), ffn_weights(rest_other, 3 * hid + ATT)]

    chooser = jnp.eye(8, OUT_PAD - OUT_HALF, dtype=BF)
    gains = by_columns(chooser, att_mine[0][1][:, OUT_HALF:])
    gain_ones = [gains[layer : layer + 1] for layer in range(layers)]
    gain_twos = [gains[layers + layer : layers + layer + 1] for layer in range(layers)]

    cosine, sine = rope_tables(positions)
    stamps = gather_group(jnp.stack([segment_ids, positions], axis=1))
    segment_all, position_all = stamps[:, 0], stamps[:, 1]
    visible = (segment_ids[:, None] == segment_all[None, :]) & (
        position_all[None, :] <= positions[:, None]
    )
    stream = pad_features(tokens)
    saved = []
    for layer in range(layers):
        qkv_m, out_m = att_mine[layer]
        qkv_o, out_o = att_other[layer]
        gu_m, down_m = ffn_mine[layer]
        gu_o, down_o = ffn_other[layer]
        normed_one, scale_one = rms_forward(stream, gain_ones[layer])
        normed_one = normed_one.astype(BF)
        qkv = join(
            product(normed_one, qkv_m)[:, :QKV_HALF], product(normed_one, qkv_o)[:, :QKV_HALF]
        )
        turned = rotate(qkv[:, : QW + KVW], cosine, sine, 1.0).astype(BF)
        query = turned[:, :QW]
        key_value = jnp.concatenate([turned[:, QW:], qkv[:, QW + KVW :].astype(BF)], axis=1)
        key_value = gather_group(key_value)
        key_all, value_all = key_value[:, :KVW], key_value[:, KVW:]
        attended, log_totals = attention(query, key_all, value_all, visible)
        att_m, att_o = halves(attended, OUT_HALF)
        mixed = (
            stream
            + by_columns(att_m, out_m[:, :OUT_HALF])
            + by_columns(att_o, out_o[:, :OUT_HALF])
        )
        normed_two, scale_two = rms_forward(mixed, gain_twos[layer])
        normed_two = normed_two.astype(BF)
        normed_pair = jnp.concatenate([normed_two, swap(normed_two, "tp")], axis=0)
        hiddens = []
        kept = []
        for weight in (gu_m, gu_o):
            both = product(normed_pair, weight)
            gate, up_value = both[:, :hid], both[:, hid:]
            sigma = jax.nn.sigmoid(gate)
            hidden = (gate * sigma * up_value).astype(BF)
            hiddens.append(hidden)
            kept.append((gate, up_value, hidden))
        partial = by_columns(hiddens[0], down_m) + by_columns(hiddens[1], down_o)
        saved.append(
            (
                stream,
                scale_one,
                normed_one,
                query,
                key_all,
                value_all,
                log_totals,
                att_m,
                att_o,
                mixed,
                scale_two,
                normed_pair,
                kept,
            )
        )
        stream = mixed + partial[:rows] + swap(partial[rows:].astype(BF), "tp").astype(F32)
    block_out = cut_features(stream)

    grad_stream = pad_features(cotangent)
    results = [None] * layers
    for layer in reversed(range(layers)):
        qkv_m, out_m = att_mine[layer]
        qkv_o, out_o = att_other[layer]
        gu_m, down_m = ffn_mine[layer]
        gu_o, down_o = ffn_other[layer]
        (
            layer_input,
            scale_one,
            normed_one,
            query,
            key_all,
            value_all,
            log_totals,
            att_m,
            att_o,
            mixed,
            scale_two,
            normed_pair,
            kept,
        ) = saved[layer]
        grad_out_b = grad_stream.astype(BF)
        grad_pair = jnp.concatenate([grad_out_b, swap(grad_out_b, "tp")], axis=0)
        partial = 0.0
        ffn_grads = []
        for (gate, up_value, hidden), gu, down in (
            (kept[0], gu_m, down_m),
            (kept[1], gu_o, down_o),
        ):
            grad_hidden = product(grad_pair, down)
            sigma = jax.nn.sigmoid(gate)
            grad_up_in = (grad_hidden * gate * sigma).astype(BF)
            grad_gate_in = (
                grad_hidden * up_value * sigma * (1.0 + gate * (1.0 - sigma))
            ).astype(BF)
            grad_gu = jnp.concatenate([grad_gate_in, grad_up_in], axis=1)
            partial = partial + by_columns(grad_gu, gu)
            ffn_grads.append(
                jnp.concatenate(
                    [
                        by_rows(normed_pair, grad_gu).astype(BF),
                        by_rows(grad_pair, hidden).astype(BF),
                    ],
                    axis=1,
                )
            )
        grad_normed_two = partial[:rows] + swap(partial[rows:].astype(BF), "tp").astype(F32)
        grad_mixed_norm, gain_two_column = rms_backward(
            mixed, scale_two, gain_twos[layer], grad_normed_two
        )
        grad_mixed = grad_stream + grad_mixed_norm
        grad_mixed_b = grad_mixed.astype(BF)
        grad_attended_b = join(
            product(grad_mixed_b, out_m)[:, :OUT_HALF], product(grad_mixed_b, out_o)[:, :OUT_HALF]
        ).astype(BF)
        out_grads = [
            jnp.concatenate(
                [by_rows(grad_mixed_b, att), gain_two_column * weight], axis=1
            ).astype(BF)
            for att, weight in ((att_m, 1.0), (att_o, 1.0))
        ]
        grad_query, key_value_terms = attention_back(
            query, key_all, value_all, visible, log_totals, grad_attended_b
        )
        key_value_grad = scatter_group(key_value_terms)
        grad_qkv = jnp.concatenate(
            [
                rotate(
                    jnp.concatenate([grad_query, key_value_grad[:, :KVW]], axis=1),
                    cosine,
                    sine,
                    -1.0,
                ),
                key_value_grad[:, KVW:],
            ],
            axis=1,
        ).astype(BF)
        grad_m, grad_o = halves(grad_qkv, QKV_HALF)
        wide = ((0, 0), (0, QKV_PAD - QKV_HALF))
        grad_m, grad_o = jnp.pad(grad_m, wide), jnp.pad(grad_o, wide)
        grad_normed_one = by_columns(grad_m, qkv_m) + by_columns(grad_o, qkv_o)
        grad_input_norm, gain_one_column = rms_backward(
            layer_input, scale_one, gain_ones[layer], grad_normed_one
        )
        grad_stream = grad_mixed + grad_input_norm
        qkv_grads = [
            jnp.concatenate(
                [
                    by_rows(normed_one, part[:, :QKV_HALF]),
                    gain_one_column,
                    jnp.zeros((DP, QKV_PAD - QKV_HALF - OUT_PAD + OUT_HALF), F32),
                ],
                axis=1,
            ).astype(BF)
            for part in (grad_m, grad_o)
        ]
        one = reduce_grads(
            jnp.concatenate([out_grads[0], ffn_grads[0]], axis=1),
            jnp.concatenate([out_grads[1], ffn_grads[1]], axis=1),
            1152,
            OUT_PAD,
        )
        two = reduce_grads(qkv_grads[0], qkv_grads[1], 512, QKV_PAD)
        results[layer] = (finish(one, OUT_PAD), finish(two, QKV_PAD))

    stacked = [[] for _ in range(9)]
    for layer in range(layers):
        (one_m, one_o), (two_m, two_o) = results[layer]
        qkv = join(two_m[:PER, :QKV_HALF], two_o[:PER, :QKV_HALF]).astype(F32)
        out = join(one_m[:PER, :OUT_HALF], one_o[:PER, :OUT_HALF]).astype(F32)
        gain_one = jnp.where(first_core, two_m[:PER, QKV_HALF], two_o[:PER, QKV_HALF])
        gain_two = jnp.where(first_core, one_m[:PER, OUT_HALF], one_o[:PER, OUT_HALF])
        ffn = [
            join(
                one_m[:PER, OUT_PAD + at * hid : OUT_PAD + (at + 1) * hid],
                one_o[:PER, OUT_PAD + at * hid : OUT_PAD + (at + 1) * hid],
            ).astype(F32)
            for at in range(3)
        ]
        for at, value in enumerate(
            [
                gain_one.astype(F32),
                qkv[:, :QW],
                qkv[:, QW : QW + KVW],
                qkv[:, QW + KVW :],
                out,
                gain_two.astype(F32),
            ]
            + ffn
        ):
            stacked[at].append(value)
    return (block_out, cut_features(grad_stream)) + tuple(jnp.stack(part) for part in stacked)


def solution(mesh):
    fine = Mesh(mesh.devices.reshape(Y, X, ZL, CORE, TP), ("y", "x", "zl", "core", "tp"))
    every = ("y", "x", "zl", "core", "tp")
    return jax.shard_map(
        shards,
        mesh=fine,
        in_specs=(
            P(every, None),
            P(every),
            P(every),
            P(every, None),
            P(None, XY),
            P(None, XY, None),
            P(None, XY, None),
            P(None, XY, None),
            P(None, XY, None),
            P(None, XY),
            P(None, XY, "tp"),
            P(None, XY, "tp"),
            P(None, XY, "tp"),
        ),
        out_specs=(
            P(every, None),
            P(every, None),
            P(None, XY),
            P(None, XY, None),
            P(None, XY, None),
            P(None, XY, None),
            P(None, XY, None),
            P(None, XY),
            P(None, XY, "tp"),
            P(None, XY, "tp"),
            P(None, XY, "tp"),
        ),
        check_vma=False,
    )
```

```python
import jax
import jax.numpy as jnp
from jax import lax
from jax.experimental import pallas as pl
from jax.experimental.pallas import tpu as pltpu
from jax.sharding import Mesh, PartitionSpec as P

D = 960
HEADS = 15
KV_HEADS = 5
HEAD = 64
QW = HEADS * HEAD
KVW = KV_HEADS * HEAD

EPSILON = 1e-05
THETA = 100000.0
MASKED = -1e30

Y, X, ZL, CORE, TP = 4, 4, 2, 2, 2
XY = ("y", "x")
PER = D // (Y * X)
PAD = 64
DP = PAD * Y * X
QKV_HALF = (QW + 2 * KVW) // 2
QKV_PAD = 896
OUT_HALF = QW // 2
OUT_PAD = 512
ATT = QKV_PAD + OUT_PAD
BF = jnp.bfloat16
F32 = jnp.float32


def product(left, right):
    return jnp.dot(left, right, preferred_element_type=F32)


def by_rows(left, right):
    return lax.dot_general(left, right, (((0,), (0,)), ((), ())), preferred_element_type=F32)


def by_columns(left, right):
    return lax.dot_general(left, right, (((1,), (1,)), ((), ())), preferred_element_type=F32)


def ring(size, step):
    return [(i, (i + step) % size) for i in range(size)]


def z_ring(step):
    pairs = []
    for low in range(ZL):
        for high in range(TP):
            there = (high * ZL + low + step) % (ZL * TP)
            pairs.append((low * TP + high, (there % ZL) * TP + there // ZL))
    return pairs


def swap(values, axis):
    return lax.ppermute(values, axis, [(0, 1), (1, 0)])


def z_send(values, step):
    return lax.ppermute(values, ("zl", "tp"), z_ring(step))


STEPS = (2, 1, 3)


def gather_group(values):
    mine = jnp.concatenate([values] + [z_send(values, step) for step in STEPS], axis=0)
    return jnp.concatenate([mine, swap(mine, "core")], axis=0)


def scatter_group(terms):
    half = terms.shape[0] // 2
    rows = half // 4
    total = terms[:half].astype(F32) + swap(terms[half:].astype(BF), "core").astype(F32)
    out = total[:rows]
    for at, step in enumerate(STEPS):
        block = total[(at + 1) * rows : (at + 2) * rows].astype(BF)
        out = out + z_send(block, -step).astype(F32)
    return out


def line_scatter(values, axis):
    at = lax.axis_index(axis)
    out = lax.dynamic_index_in_dim(values, at, 0, False).astype(F32)
    for step in STEPS:
        block = lax.dynamic_index_in_dim(values, (at + step) % 4, 0, False)
        out = out + lax.ppermute(block, axis, ring(4, step)).astype(F32)
    return out


def plane_scatter(values, cut):
    view = values.reshape(Y, X, PAD, values.shape[1])
    first = line_scatter(jnp.swapaxes(view[..., :cut], 0, 1), "x").astype(BF)
    second = line_scatter(view[..., cut:], "y").astype(BF)
    first = line_scatter(first, "y")
    second = line_scatter(second, "x")
    return jnp.concatenate([first, second], axis=1)


def core_sum(keep, give):
    return (keep.astype(F32) + swap(give.astype(BF), "core").astype(F32)).astype(BF)


def low_sum(part):
    part = part.astype(BF)
    return (part.astype(F32) + swap(part, "zl").astype(F32)).astype(BF)


def diagonal(lefts, rights):
    tall = jnp.concatenate(lefts, axis=0)
    width = sum(right.shape[1] for right in rights)
    blocks, at = [], 0
    for right in rights:
        left_over = width - at - right.shape[1]
        blocks.append(jnp.pad(right, ((0, 0), (at, left_over))))
        at += right.shape[1]
    return by_rows(tall, jnp.concatenate(blocks, axis=0)).astype(BF)


def finish(total, tp_width):
    part = total[:, :tp_width]
    part = (part.astype(F32) + swap(part, "tp").astype(F32)).astype(BF)
    if tp_width < total.shape[1]:
        part = jnp.concatenate([part, total[:, tp_width:]], axis=1)
    return part, swap(part, "core")


def scatter_plane(total):
    return lax.psum_scatter(total, XY, scatter_dimension=0, tiled=True)


def rope_tables(positions):
    half_head = HEAD // 2
    freqs = THETA ** (-2.0 * jnp.arange(half_head, dtype=F32) / HEAD)
    angles = positions.astype(F32)[:, None] * freqs[None, :]
    return (jnp.cos(angles), jnp.sin(angles))


def rotate(values, cosine, sine, direction):
    row_count = values.shape[0]
    split_view = values.reshape(row_count, -1, 2, HEAD // 2)
    first_half = split_view[:, :, 0]
    second_half = split_view[:, :, 1]
    cos_rows = cosine[:, None, :]
    sin_rows = direction * sine[:, None, :]
    turned = jnp.stack(
        [
            first_half * cos_rows - second_half * sin_rows,
            second_half * cos_rows + first_half * sin_rows,
        ],
        axis=2,
    )
    return turned.reshape(row_count, -1)


def rms_forward(values, gain):
    mean = jnp.sum(values * values, axis=-1, keepdims=True) * (1.0 / D)
    scale = lax.rsqrt(mean + EPSILON)
    return (values * scale * gain, scale)


def rms_backward(values, scale, gain, grad_normed):
    weighted = grad_normed * gain
    mean = jnp.sum(weighted * values, axis=-1, keepdims=True) * (1.0 / D)
    grad_values = scale * weighted - values * (scale * scale * scale) * mean
    return (grad_values, (grad_normed * values * scale).astype(BF))


SHARE = HEADS // KV_HEADS
VM = pl.BlockSpec(memory_space=pltpu.VMEM)


def head_stack(ref, group):
    return jnp.concatenate(
        [
            ref[:, (group * SHARE + at) * HEAD : (group * SHARE + at + 1) * HEAD]
            for at in range(SHARE)
        ],
        axis=0,
    )


def mask_bias(codes):
    segment_q, position_q, segment_k, position_k = codes
    seen = (segment_k[...] == segment_q[...]) & (position_k[...] <= position_q[...])
    return jnp.where(seen, 0.0, MASKED)


def attend_kernel(q_ref, kv_ref, sq, pq, sk, pk, att_ref, lse_ref, bias_ref):
    rows = q_ref.shape[0]
    bias_ref[...] = mask_bias((sq, pq, sk, pk))
    for group in range(KV_HEADS):
        query = head_stack(q_ref, group) * BF(HEAD ** (-0.5))
        key = kv_ref[:, group * HEAD : (group + 1) * HEAD]
        value = kv_ref[:, KVW + group * HEAD : KVW + (group + 1) * HEAD]
        scores = by_columns(key, query) + bias_ref[...]
        top = jnp.max(scores, axis=0, keepdims=True)
        terms = jnp.exp(scores - top)
        total = jnp.sum(terms, axis=0, keepdims=True)
        lse_ref[group : group + 1, :] = top + jnp.log(total)
        out = (by_rows(value, terms.astype(BF)) * (1.0 / total)).T
        for at in range(SHARE):
            head = group * SHARE + at
            att_ref[:, head * HEAD : (head + 1) * HEAD] = out[
                at * rows : (at + 1) * rows
            ].astype(BF)


def attend_back_kernel(
    q_ref, kv_ref, da_ref, lse_ref, sq, pq, sk, pk, dq_ref, dkv_ref, bias_ref
):
    rows = q_ref.shape[0]
    bias_ref[...] = mask_bias((sq, pq, sk, pk))
    for group in range(KV_HEADS):
        query = head_stack(q_ref, group) * BF(HEAD ** (-0.5))
        grad = head_stack(da_ref, group)
        key = kv_ref[:, group * HEAD : (group + 1) * HEAD]
        value = kv_ref[:, KVW + group * HEAD : KVW + (group + 1) * HEAD]
        probs = jnp.exp(by_columns(key, query) + bias_ref[...] - lse_ref[group : group + 1, :])
        grad_probs = by_columns(value, grad)
        delta = jnp.sum(probs * grad_probs, axis=0, keepdims=True)
        grad_scores = (probs * (grad_probs - delta)).astype(BF)
        dkv_ref[:, group * HEAD : (group + 1) * HEAD] = product(grad_scores, query).astype(BF)
        dkv_ref[:, KVW + group * HEAD : KVW + (group + 1) * HEAD] = product(
            probs.astype(BF), grad
        ).astype(BF)
        out = (by_rows(key, grad_scores) * (HEAD ** (-0.5))).T
        for at in range(SHARE):
            head = group * SHARE + at
            dq_ref[:, head * HEAD : (head + 1) * HEAD] = out[at * rows : (at + 1) * rows]


def attention(query, key_value, codes):
    rows, keys = query.shape[0], key_value.shape[0]
    return pl.pallas_call(
        attend_kernel,
        out_shape=(
            jax.ShapeDtypeStruct((rows, QW), BF),
            jax.ShapeDtypeStruct((8, SHARE * rows), F32),
        ),
        in_specs=[VM] * 6,
        out_specs=(VM, VM),
        scratch_shapes=[pltpu.VMEM((keys, SHARE * rows), F32)],
        compiler_params=pltpu.CompilerParams(vmem_limit_bytes=40 * 2**20),
        cost_estimate=pl.CostEstimate(
            flops=16 * HEADS * HEAD * rows * keys,
            bytes_accessed=4 * 2**20,
            transcendentals=HEADS * rows * keys,
        ),
        name="attend",
    )(query, key_value, *codes)


def attention_back(query, key_value, grad_attended_b, log_totals, codes):
    rows, keys = query.shape[0], key_value.shape[0]
    return pl.pallas_call(
        attend_back_kernel,
        out_shape=(
            jax.ShapeDtypeStruct((rows, QW), F32),
            jax.ShapeDtypeStruct((keys, 2 * KVW), BF),
        ),
        in_specs=[VM] * 8,
        out_specs=(VM, VM),
        scratch_shapes=[pltpu.VMEM((keys, SHARE * rows), F32)],
        compiler_params=pltpu.CompilerParams(vmem_limit_bytes=48 * 2**20),
        cost_estimate=pl.CostEstimate(
            flops=40 * HEADS * HEAD * rows * keys,
            bytes_accessed=6 * 2**20,
            transcendentals=HEADS * rows * keys,
        ),
        name="attend_back",
    )(query, key_value, grad_attended_b, log_totals, *codes)


def pad_features(values):
    rows = values.shape[0]
    view = values.reshape(rows, Y * X, PER)
    return jnp.pad(view, ((0, 0), (0, 0), (0, PAD - PER))).reshape(rows, DP)


def cut_features(values):
    rows = values.shape[0]
    return values.reshape(rows, Y * X, PAD)[:, :, :PER].reshape(rows, D)


def shards(
    tokens,
    segment_ids,
    positions,
    cotangent,
    attn_gain,
    w_query,
    w_key,
    w_value,
    w_out,
    ffn_gain,
    w_gate,
    w_up,
    w_down,
):
    layers = attn_gain.shape[0]
    rows = tokens.shape[0]
    hid = w_gate.shape[2] // 2
    first_core = lax.axis_index("core") == 0

    def pick(low, high):
        return jnp.where(first_core, low, high), jnp.where(first_core, high, low)

    def halves(whole, width):
        return pick(whole[..., :width], whole[..., width:])

    def join(mine, other):
        low, high = pick(mine, other)
        return jnp.concatenate([low, high], axis=-1)

    def tall(values):
        return jnp.pad(values, ((0, PAD - PER), (0, 0)))

    gain_columns = jnp.stack(
        [attn_gain[layer] for layer in range(layers)] + [ffn_gain[layer] for layer in range(layers)],
        axis=1,
    )
    gain_columns = jnp.pad(gain_columns, ((0, 0), (0, OUT_PAD - OUT_HALF - 2 * layers)))
    packs = []
    for layer in range(layers):
        qkv = jnp.concatenate([w_query[layer], w_key[layer], w_value[layer]], axis=1)
        qkv_mine = jnp.pad(halves(qkv, QKV_HALF)[0], ((0, 0), (0, QKV_PAD - QKV_HALF)))
        out_mine = halves(w_out[layer], OUT_HALF)[0]
        packs.append(jnp.concatenate([qkv_mine, out_mine, gain_columns], axis=1))
        packs.append(
            jnp.concatenate(
                [halves(w[layer], hid)[0] for w in (w_gate, w_up, w_down)], axis=1
            )
        )
    packs = [tall(pack) for pack in packs]
    att_mine, att_other, ffn_mine, ffn_other = [], [], [], []
    for layer in range(layers):
        whole = lax.all_gather(
            jnp.concatenate(packs[2 * layer : 2 * layer + 2], axis=1), XY, axis=0, tiled=True
        )
        att = whole[:, :ATT]
        ffn = whole[:, ATT:]
        for part, att_list, ffn_list in (
            ((att, ffn), att_mine, ffn_mine),
            ((swap(att, "core"), swap(ffn, "core")), att_other, ffn_other),
        ):
            att_list.append((part[0][:, :QKV_PAD], part[0][:, QKV_PAD:]))
            ffn_list.append((part[1][:, : 2 * hid], part[1][:, 2 * hid :]))

    chooser = jnp.eye(8, OUT_PAD - OUT_HALF, dtype=BF)
    gains = by_columns(chooser, att_mine[0][1][:, OUT_HALF:])
    gain_ones = [gains[layer : layer + 1] for layer in range(layers)]
    gain_twos = [gains[layers + layer : layers + layer + 1] for layer in range(layers)]

    cosine, sine = rope_tables(positions)
    stamps = gather_group(jnp.stack([segment_ids, positions], axis=1))
    codes = (
        jnp.tile(segment_ids, SHARE)[None, :],
        jnp.tile(positions, SHARE)[None, :],
        stamps[:, :1],
        stamps[:, 1:],
    )
    stream = pad_features(tokens)
    saved = []
    for layer in range(layers):
        qkv_m, out_m = att_mine[layer]
        qkv_o, out_o = att_other[layer]
        gu_m, down_m = ffn_mine[layer]
        gu_o, down_o = ffn_other[layer]
        normed_one, scale_one = rms_forward(stream, gain_ones[layer])
        normed_one = normed_one.astype(BF)
        qkv = join(
            product(normed_one, qkv_m)[:, :QKV_HALF], product(normed_one, qkv_o)[:, :QKV_HALF]
        )
        turned = rotate(qkv[:, : QW + KVW], cosine, sine, 1.0).astype(BF)
        query = turned[:, :QW]
        key_value = jnp.concatenate([turned[:, QW:], qkv[:, QW + KVW :].astype(BF)], axis=1)
        key_value = gather_group(key_value)
        attended, log_totals = attention(query, key_value, codes)
        att_m, att_o = halves(attended, OUT_HALF)
        mixed = (
            stream
            + by_columns(att_m, out_m[:, :OUT_HALF])
            + by_columns(att_o, out_o[:, :OUT_HALF])
        )
        normed_two, scale_two = rms_forward(mixed, gain_twos[layer])
        normed_two = normed_two.astype(BF)
        normed_pair = jnp.concatenate([normed_two, swap(normed_two, "tp")], axis=0)
        hiddens = []
        kept = []
        for weight in (gu_m, gu_o):
            both = product(normed_pair, weight)
            gate, up_value = both[:, :hid], both[:, hid:]
            sigma = jax.nn.sigmoid(gate)
            hidden = (gate * sigma * up_value).astype(BF)
            hiddens.append(hidden)
            kept.append((gate, up_value, hidden))
        partial = by_columns(hiddens[0], down_m) + by_columns(hiddens[1], down_o)
        saved.append(
            (
                stream,
                scale_one,
                normed_one,
                query,
                key_value,
                log_totals,
                att_m,
                att_o,
                mixed,
                scale_two,
                normed_pair,
                kept,
            )
        )
        stream = mixed + partial[:rows] + swap(partial[rows:].astype(BF), "tp").astype(F32)
    block_out = cut_features(stream)

    grad_stream = pad_features(cotangent)
    results = [None] * layers
    for layer in reversed(range(layers)):
        qkv_m, out_m = att_mine[layer]
        qkv_o, out_o = att_other[layer]
        gu_m, down_m = ffn_mine[layer]
        gu_o, down_o = ffn_other[layer]
        (
            layer_input,
            scale_one,
            normed_one,
            query,
            key_value,
            log_totals,
            att_m,
            att_o,
            mixed,
            scale_two,
            normed_pair,
            kept,
        ) = saved[layer]
        grad_out_b = grad_stream.astype(BF)
        grad_pair = jnp.concatenate([grad_out_b, swap(grad_out_b, "tp")], axis=0)
        partial = 0.0
        ffn_grads = []
        for (gate, up_value, hidden), gu, down in (
            (kept[0], gu_m, down_m),
            (kept[1], gu_o, down_o),
        ):
            grad_hidden = product(grad_pair, down)
            sigma = jax.nn.sigmoid(gate)
            grad_up_in = (grad_hidden * gate * sigma).astype(BF)
            grad_gate_in = (
                grad_hidden * up_value * sigma * (1.0 + gate * (1.0 - sigma))
            ).astype(BF)
            grad_gu = jnp.concatenate([grad_gate_in, grad_up_in], axis=1)
            partial = partial + by_columns(grad_gu, gu)
            ffn_grads.append(diagonal([normed_pair, grad_pair], [grad_gu, hidden]))
        arrived = swap(partial[rows:].astype(BF), "tp")
        if layer == 0:
            arrived, ffn_grads, pending = lax.optimization_barrier((arrived, ffn_grads, pending))
            later = scatter_plane(pending)
            ffn_sum = core_sum(ffn_grads[0], ffn_grads[1])
        grad_normed_two = partial[:rows] + arrived.astype(F32)
        grad_mixed_norm, gain_two_terms = rms_backward(
            mixed, scale_two, gain_twos[layer], grad_normed_two
        )
        grad_mixed = grad_stream + grad_mixed_norm
        grad_mixed_b = grad_mixed.astype(BF)
        grad_attended_b = join(
            product(grad_mixed_b, out_m)[:, :OUT_HALF], product(grad_mixed_b, out_o)[:, :OUT_HALF]
        ).astype(BF)
        grad_query, key_value_terms = attention_back(
            query, key_value, grad_attended_b, log_totals, codes
        )
        if layer == 0:
            ffn_sum, key_value_terms = lax.optimization_barrier((ffn_sum, key_value_terms))
            ffn_sum = plane_scatter(ffn_sum, 1024)
        key_value_grad = scatter_group(key_value_terms)
        grad_qkv = jnp.concatenate(
            [
                rotate(
                    jnp.concatenate([grad_query, key_value_grad[:, :KVW]], axis=1),
                    cosine,
                    sine,
                    -1.0,
                ),
                key_value_grad[:, KVW:],
            ],
            axis=1,
        ).astype(BF)
        grad_m, grad_o = halves(grad_qkv, QKV_HALF)
        wide = ((0, 0), (0, QKV_PAD - QKV_HALF))
        grad_m, grad_o = jnp.pad(grad_m, wide), jnp.pad(grad_o, wide)
        grad_normed_one = by_columns(grad_m, qkv_m) + by_columns(grad_o, qkv_o)
        grad_input_norm, gain_one_terms = rms_backward(
            layer_input, scale_one, gain_ones[layer], grad_normed_one
        )
        grad_stream = grad_mixed + grad_input_norm
        ones = jnp.ones((rows, OUT_PAD - OUT_HALF), BF)
        att_grads = [
            diagonal(
                [normed_one, gain_one_terms, grad_mixed_b, gain_two_terms],
                [
                    grad_part[:, :QKV_HALF],
                    jnp.ones((rows, QKV_PAD - QKV_HALF), BF),
                    att_part,
                    ones,
                ],
            )
            for grad_part, att_part in ((grad_m, att_m), (grad_o, att_o))
        ]
        if layer > 0:
            grad_stream, keep, give = lax.optimization_barrier(
                (
                    grad_stream,
                    jnp.concatenate([att_grads[0], ffn_grads[0]], axis=1),
                    jnp.concatenate([att_grads[1], ffn_grads[1]], axis=1),
                )
            )
            pending = core_sum(keep, give)
        else:
            later = low_sum(later)
            ffn_sum = low_sum(ffn_sum)
            att_sum = low_sum(plane_scatter(core_sum(att_grads[0], att_grads[1]), 768))
            results[1] = finish(later, ATT)
            results[0] = finish(jnp.concatenate([att_sum, ffn_sum], axis=1), ATT)

    stacked = [[] for _ in range(9)]
    for layer in range(layers):
        mine, other = results[layer]
        mine, other = mine[:PER], other[:PER]
        qkv = join(mine[:, :QKV_HALF], other[:, :QKV_HALF]).astype(F32)
        out = join(
            mine[:, QKV_PAD : QKV_PAD + OUT_HALF], other[:, QKV_PAD : QKV_PAD + OUT_HALF]
        ).astype(F32)
        gain_one = pick(mine[:, QKV_HALF], other[:, QKV_HALF])[0]
        gain_two = pick(mine[:, QKV_PAD + OUT_HALF], other[:, QKV_PAD + OUT_HALF])[0]
        ffn = [
            join(
                mine[:, ATT + at * hid : ATT + (at + 1) * hid],
                other[:, ATT + at * hid : ATT + (at + 1) * hid],
            ).astype(F32)
            for at in range(3)
        ]
        for at, value in enumerate(
            [
                gain_one.astype(F32),
                qkv[:, :QW],
                qkv[:, QW : QW + KVW],
                qkv[:, QW + KVW :],
                out,
                gain_two.astype(F32),
            ]
            + ffn
        ):
            stacked[at].append(value)
    return (block_out, cut_features(grad_stream)) + tuple(jnp.stack(part) for part in stacked)


def solution(mesh):
    fine = Mesh(mesh.devices.reshape(Y, X, ZL, CORE, TP), ("y", "x", "zl", "core", "tp"))
    every = ("y", "x", "zl", "core", "tp")
    return jax.shard_map(
        shards,
        mesh=fine,
        in_specs=(
            P(every, None),
            P(every),
            P(every),
            P(every, None),
            P(None, XY),
            P(None, XY, None),
            P(None, XY, None),
            P(None, XY, None),
            P(None, XY, None),
            P(None, XY),
            P(None, XY, "tp"),
            P(None, XY, "tp"),
            P(None, XY, "tp"),
        ),
        out_specs=(
            P(every, None),
            P(every, None),
            P(None, XY),
            P(None, XY, None),
            P(None, XY, None),
            P(None, XY, None),
            P(None, XY, None),
            P(None, XY),
            P(None, XY, "tp"),
            P(None, XY, "tp"),
            P(None, XY, "tp"),
        ),
        check_vma=False,
    )
```

```python
import jax
import jax.numpy as jnp
from jax import lax
from jax.experimental import pallas as pl
from jax.experimental.pallas import tpu as pltpu
from jax.sharding import Mesh, PartitionSpec as P

D = 960
HEADS = 15
KV_HEADS = 5
HEAD = 64
QW = HEADS * HEAD
KVW = KV_HEADS * HEAD

EPSILON = 1e-05
THETA = 100000.0
MASKED = -1e30

Y, X, ZL, CORE, TP = 4, 4, 2, 2, 2
XY = ("y", "x")
PER = D // (Y * X)
PAD = 64
DP = PAD * Y * X
QKV_HALF = (QW + 2 * KVW) // 2
QKV_PAD = 896
OUT_HALF = QW // 2
OUT_PAD = 512
ATT = QKV_PAD + OUT_PAD
BF = jnp.bfloat16
VM = pl.BlockSpec(memory_space=pltpu.VMEM)
F32 = jnp.float32


def product(left, right):
    return jnp.dot(left, right, preferred_element_type=F32)


def by_rows(left, right):
    return lax.dot_general(left, right, (((0,), (0,)), ((), ())), preferred_element_type=F32)


def by_columns(left, right):
    return lax.dot_general(left, right, (((1,), (1,)), ((), ())), preferred_element_type=F32)


def ring(size, step):
    return [(i, (i + step) % size) for i in range(size)]


def z_ring(step):
    pairs = []
    for low in range(ZL):
        for high in range(TP):
            there = (high * ZL + low + step) % (ZL * TP)
            pairs.append((low * TP + high, (there % ZL) * TP + there // ZL))
    return pairs


def swap(values, axis):
    return lax.ppermute(values, axis, [(0, 1), (1, 0)])


def z_send(values, step):
    return lax.ppermute(values, ("zl", "tp"), z_ring(step))


STEPS = (2, 1, 3)


def gather_group(values):
    mine = jnp.concatenate([values] + [z_send(values, step) for step in STEPS], axis=0)
    return jnp.concatenate([mine, swap(mine, "core")], axis=0)


def scatter_group(terms):
    half = terms.shape[0] // 2
    rows = half // 4
    total = terms[:half].astype(F32) + swap(terms[half:].astype(BF), "core").astype(F32)
    out = total[:rows]
    for at, step in enumerate(STEPS):
        block = total[(at + 1) * rows : (at + 2) * rows].astype(BF)
        out = out + z_send(block, -step).astype(F32)
    return out


def line_scatter(values, axis):
    at = lax.axis_index(axis)
    out = lax.dynamic_index_in_dim(values, at, 0, False).astype(F32)
    for step in STEPS:
        block = lax.dynamic_index_in_dim(values, (at + step) % 4, 0, False)
        out = out + lax.ppermute(block, axis, ring(4, step)).astype(F32)
    return out


def plane_scatter(values, cut):
    view = values.reshape(Y, X, PAD, values.shape[1])
    first = line_scatter(jnp.swapaxes(view[..., :cut], 0, 1), "x").astype(BF)
    second = line_scatter(view[..., cut:], "y").astype(BF)
    first = line_scatter(first, "y")
    second = line_scatter(second, "x")
    return jnp.concatenate([first, second], axis=1)


def core_sum(keep, give):
    return (keep.astype(F32) + swap(give.astype(BF), "core").astype(F32)).astype(BF)


def low_sum(part):
    part = part.astype(BF)
    return (part.astype(F32) + swap(part, "zl").astype(F32)).astype(BF)


def z_sum(part):
    part = part.astype(BF)
    two, one, three = (z_send(part, step).astype(F32) for step in STEPS)
    return ((part.astype(F32) + two) + (one + three)).astype(BF)


def merge_kernel(a_ref, b_ref, c_ref, d_ref, out_ref):
    width = a_ref.shape[1]
    out_ref[:, :width] = (a_ref[...].astype(F32) + b_ref[...].astype(F32)).astype(BF)
    out_ref[:, width:] = (c_ref[...].astype(F32) + d_ref[...].astype(F32)).astype(BF)


def merge_sum(first, second):
    left, right = first[0].shape[1], second[0].shape[1]
    block = 128
    narrow = pl.BlockSpec((block, left), lambda i: (i, 0))
    broad = pl.BlockSpec((block, right), lambda i: (i, 0))
    return pl.pallas_call(
        merge_kernel,
        grid=(DP // block,),
        out_shape=jax.ShapeDtypeStruct((DP, left + right), BF),
        in_specs=[narrow, narrow, broad, broad],
        out_specs=pl.BlockSpec((block, left + right), lambda i: (i, 0)),
        cost_estimate=pl.CostEstimate(
            flops=2 * DP * (left + right),
            bytes_accessed=6 * DP * (left + right),
            transcendentals=0,
        ),
        name="merge_sum",
    )(first[0], swap(first[1], "core"), second[0], swap(second[1], "core"))


def write_kernel(flag_ref, m0, o0, m1, o1, q_ref, k_ref, v_ref, w_ref, gain_ref, qkv_ref, out_ref):
    first = flag_ref[0] == 0
    chooser = (
        lax.broadcasted_iota(jnp.int32, (8, OUT_PAD - OUT_HALF), 0)
        == lax.broadcasted_iota(jnp.int32, (8, OUT_PAD - OUT_HALF), 1)
    ).astype(BF)
    for layer, (mine, other) in enumerate(((m0, o0), (m1, o1))):
        low = jnp.where(first, mine[...], other[...]).astype(F32)
        high = jnp.where(first, other[...], mine[...]).astype(F32)
        qkv_ref[:, :QKV_HALF] = low[:, :QKV_HALF]
        qkv_ref[:, QKV_HALF:] = high[:, :QKV_HALF]
        out_ref[:, :OUT_HALF] = low[:, QKV_PAD : QKV_PAD + OUT_HALF]
        out_ref[:, OUT_HALF:] = high[:, QKV_PAD : QKV_PAD + OUT_HALF]
        q_ref[layer] = qkv_ref[:PER, :QW]
        k_ref[layer] = qkv_ref[:PER, QW : QW + KVW]
        v_ref[layer] = qkv_ref[:PER, QW + KVW :]
        w_ref[layer] = out_ref[:PER, :]
        low = low.astype(BF)
        for at, start in enumerate((QKV_HALF, QKV_PAD + OUT_HALF)):
            gain_ref[at * 2 + layer] = by_columns(
                chooser, low[:, start : start + OUT_PAD - OUT_HALF]
            )


def write_grads(flag, parts):
    shapes = [(2, PER, QW), (2, PER, KVW), (2, PER, KVW), (2, PER, QW), (4, 8, PAD)]
    return pl.pallas_call(
        write_kernel,
        out_shape=tuple(jax.ShapeDtypeStruct(shape, F32) for shape in shapes),
        in_specs=[pl.BlockSpec(memory_space=pltpu.SMEM)] + [VM] * 4,
        out_specs=(VM,) * 5,
        scratch_shapes=[pltpu.VMEM((PAD, QW + 2 * KVW), F32), pltpu.VMEM((PAD, QW), F32)],
        compiler_params=pltpu.CompilerParams(vmem_limit_bytes=32 * 2**20),
        name="write_grads",
    )(flag, *parts)


def diagonal(lefts, rights):
    tall = jnp.concatenate(lefts, axis=0)
    width = sum(right.shape[1] for right in rights)
    blocks, at = [], 0
    for right in rights:
        left_over = width - at - right.shape[1]
        blocks.append(jnp.pad(right, ((0, 0), (at, left_over))))
        at += right.shape[1]
    return by_rows(tall, jnp.concatenate(blocks, axis=0)).astype(BF)


def scatter_plane(total):
    return lax.psum_scatter(total, XY, scatter_dimension=0, tiled=True)


def rope_tables(positions):
    half_head = HEAD // 2
    freqs = THETA ** (-2.0 * jnp.arange(half_head, dtype=F32) / HEAD)
    angles = positions.astype(F32)[:, None] * freqs[None, :]
    return (jnp.cos(angles), jnp.sin(angles))


def rotate(values, cosine, sine, direction):
    row_count = values.shape[0]
    split_view = values.reshape(row_count, -1, 2, HEAD // 2)
    first_half = split_view[:, :, 0]
    second_half = split_view[:, :, 1]
    cos_rows = cosine[:, None, :]
    sin_rows = direction * sine[:, None, :]
    turned = jnp.stack(
        [
            first_half * cos_rows - second_half * sin_rows,
            second_half * cos_rows + first_half * sin_rows,
        ],
        axis=2,
    )
    return turned.reshape(row_count, -1)


def rms_forward(values, gain):
    mean = jnp.sum(values * values, axis=-1, keepdims=True) * (1.0 / D)
    scale = lax.rsqrt(mean + EPSILON)
    return (values * scale * gain, scale)


def rms_backward(values, scale, gain, grad_normed):
    weighted = grad_normed * gain
    mean = jnp.sum(weighted * values, axis=-1, keepdims=True) * (1.0 / D)
    grad_values = scale * weighted - values * (scale * scale * scale) * mean
    return (grad_values, (grad_normed * values * scale).astype(BF))


SHARE = HEADS // KV_HEADS


def head_stack(ref, group):
    return jnp.concatenate(
        [
            ref[:, (group * SHARE + at) * HEAD : (group * SHARE + at + 1) * HEAD]
            for at in range(SHARE)
        ],
        axis=0,
    )


def mask_bias(codes):
    segment_q, position_q, segment_k, position_k = codes
    seen = (segment_k[...] == segment_q[...]) & (position_k[...] <= position_q[...])
    return jnp.where(seen, 0.0, MASKED)


def attend_kernel(q_ref, kv_ref, sq, pq, sk, pk, att_ref, lse_ref, bias_ref):
    rows = q_ref.shape[0]
    bias_ref[...] = mask_bias((sq, pq, sk, pk))
    for group in range(KV_HEADS):
        query = head_stack(q_ref, group) * BF(HEAD ** (-0.5))
        key = kv_ref[:, group * HEAD : (group + 1) * HEAD]
        value = kv_ref[:, KVW + group * HEAD : KVW + (group + 1) * HEAD]
        scores = by_columns(key, query) + bias_ref[...]
        top = jnp.max(scores, axis=0, keepdims=True)
        terms = jnp.exp(scores - top)
        total = jnp.sum(terms, axis=0, keepdims=True)
        lse_ref[group : group + 1, :] = top + jnp.log(total)
        out = (by_rows(value, terms.astype(BF)) * (1.0 / total)).T
        for at in range(SHARE):
            head = group * SHARE + at
            att_ref[:, head * HEAD : (head + 1) * HEAD] = out[
                at * rows : (at + 1) * rows
            ].astype(BF)


def attend_back_kernel(
    q_ref, kv_ref, da_ref, lse_ref, sq, pq, sk, pk, dq_ref, dkv_ref, bias_ref
):
    rows = q_ref.shape[0]
    bias_ref[...] = mask_bias((sq, pq, sk, pk))
    for group in range(KV_HEADS):
        query = head_stack(q_ref, group) * BF(HEAD ** (-0.5))
        grad = head_stack(da_ref, group)
        key = kv_ref[:, group * HEAD : (group + 1) * HEAD]
        value = kv_ref[:, KVW + group * HEAD : KVW + (group + 1) * HEAD]
        probs = jnp.exp(by_columns(key, query) + bias_ref[...] - lse_ref[group : group + 1, :])
        grad_probs = by_columns(value, grad)
        delta = jnp.sum(probs * grad_probs, axis=0, keepdims=True)
        grad_scores = (probs * (grad_probs - delta)).astype(BF)
        dkv_ref[:, group * HEAD : (group + 1) * HEAD] = product(grad_scores, query).astype(BF)
        dkv_ref[:, KVW + group * HEAD : KVW + (group + 1) * HEAD] = product(
            probs.astype(BF), grad
        ).astype(BF)
        out = (by_rows(key, grad_scores) * (HEAD ** (-0.5))).T
        for at in range(SHARE):
            head = group * SHARE + at
            dq_ref[:, head * HEAD : (head + 1) * HEAD] = out[at * rows : (at + 1) * rows]


def attention(query, key_value, codes):
    rows, keys = query.shape[0], key_value.shape[0]
    return pl.pallas_call(
        attend_kernel,
        out_shape=(
            jax.ShapeDtypeStruct((rows, QW), BF),
            jax.ShapeDtypeStruct((8, SHARE * rows), F32),
        ),
        in_specs=[VM] * 6,
        out_specs=(VM, VM),
        scratch_shapes=[pltpu.VMEM((keys, SHARE * rows), F32)],
        compiler_params=pltpu.CompilerParams(vmem_limit_bytes=40 * 2**20),
        cost_estimate=pl.CostEstimate(
            flops=16 * HEADS * HEAD * rows * keys,
            bytes_accessed=4 * 2**20,
            transcendentals=HEADS * rows * keys,
        ),
        name="attend",
    )(query, key_value, *codes)


def attention_back(query, key_value, grad_attended_b, log_totals, codes):
    rows, keys = query.shape[0], key_value.shape[0]
    return pl.pallas_call(
        attend_back_kernel,
        out_shape=(
            jax.ShapeDtypeStruct((rows, QW), F32),
            jax.ShapeDtypeStruct((keys, 2 * KVW), BF),
        ),
        in_specs=[VM] * 8,
        out_specs=(VM, VM),
        scratch_shapes=[pltpu.VMEM((keys, SHARE * rows), F32)],
        compiler_params=pltpu.CompilerParams(vmem_limit_bytes=48 * 2**20),
        cost_estimate=pl.CostEstimate(
            flops=40 * HEADS * HEAD * rows * keys,
            bytes_accessed=6 * 2**20,
            transcendentals=HEADS * rows * keys,
        ),
        name="attend_back",
    )(query, key_value, grad_attended_b, log_totals, *codes)


def pad_features(values):
    rows = values.shape[0]
    view = values.reshape(rows, Y * X, PER)
    return jnp.pad(view, ((0, 0), (0, 0), (0, PAD - PER))).reshape(rows, DP)


def cut_features(values):
    rows = values.shape[0]
    return values.reshape(rows, Y * X, PAD)[:, :, :PER].reshape(rows, D)


def shards(
    tokens,
    segment_ids,
    positions,
    cotangent,
    attn_gain,
    w_query,
    w_key,
    w_value,
    w_out,
    ffn_gain,
    w_gate,
    w_up,
    w_down,
):
    layers = attn_gain.shape[0]
    rows = tokens.shape[0]
    hid = w_gate.shape[2] // 2
    first_core = lax.axis_index("core") == 0

    def pick(low, high):
        return jnp.where(first_core, low, high), jnp.where(first_core, high, low)

    def halves(whole, width):
        return pick(whole[..., :width], whole[..., width:])

    def join(mine, other):
        low, high = pick(mine, other)
        return jnp.concatenate([low, high], axis=-1)

    def tall(values):
        return jnp.pad(values, ((0, PAD - PER), (0, 0)))

    gain_columns = jnp.stack(
        [attn_gain[layer] for layer in range(layers)] + [ffn_gain[layer] for layer in range(layers)],
        axis=1,
    )
    gain_columns = jnp.pad(gain_columns, ((0, 0), (0, OUT_PAD - OUT_HALF - 2 * layers)))
    packs = []
    for layer in range(layers):
        qkv = jnp.concatenate([w_query[layer], w_key[layer], w_value[layer]], axis=1)
        qkv_mine = jnp.pad(halves(qkv, QKV_HALF)[0], ((0, 0), (0, QKV_PAD - QKV_HALF)))
        out_mine = halves(w_out[layer], OUT_HALF)[0]
        packs.append(jnp.concatenate([qkv_mine, out_mine, gain_columns], axis=1))
        packs.append(
            jnp.concatenate(
                [halves(w[layer], hid)[0] for w in (w_gate, w_up, w_down)], axis=1
            )
        )
    packs = [tall(pack) for pack in packs]
    att_mine, att_other, ffn_mine, ffn_other = [], [], [], []
    for layer in range(layers):
        whole = lax.all_gather(
            jnp.concatenate(packs[2 * layer : 2 * layer + 2], axis=1), XY, axis=0, tiled=True
        )
        att = whole[:, :ATT]
        ffn = whole[:, ATT:]
        for part, att_list, ffn_list in (
            ((att, ffn), att_mine, ffn_mine),
            ((swap(att, "core"), swap(ffn, "core")), att_other, ffn_other),
        ):
            att_list.append((part[0][:, :QKV_PAD], part[0][:, QKV_PAD:]))
            ffn_list.append((part[1][:, : 2 * hid], part[1][:, 2 * hid :]))

    chooser = jnp.eye(8, OUT_PAD - OUT_HALF, dtype=BF)
    gains = by_columns(chooser, att_mine[0][1][:, OUT_HALF:])
    gain_ones = [gains[layer : layer + 1] for layer in range(layers)]
    gain_twos = [gains[layers + layer : layers + layer + 1] for layer in range(layers)]

    cosine, sine = rope_tables(positions)
    stamps = gather_group(jnp.stack([segment_ids, positions], axis=1))
    codes = (
        jnp.tile(segment_ids, SHARE)[None, :],
        jnp.tile(positions, SHARE)[None, :],
        stamps[:, :1],
        stamps[:, 1:],
    )
    stream = pad_features(tokens)
    saved = []
    for layer in range(layers):
        qkv_m, out_m = att_mine[layer]
        qkv_o, out_o = att_other[layer]
        gu_m, down_m = ffn_mine[layer]
        gu_o, down_o = ffn_other[layer]
        normed_one, scale_one = rms_forward(stream, gain_ones[layer])
        normed_one = normed_one.astype(BF)
        qkv = join(
            product(normed_one, qkv_m)[:, :QKV_HALF], product(normed_one, qkv_o)[:, :QKV_HALF]
        )
        turned = rotate(qkv[:, : QW + KVW], cosine, sine, 1.0).astype(BF)
        query = turned[:, :QW]
        key_value = jnp.concatenate([turned[:, QW:], qkv[:, QW + KVW :].astype(BF)], axis=1)
        key_value = gather_group(key_value)
        attended, log_totals = attention(query, key_value, codes)
        att_m, att_o = halves(attended, OUT_HALF)
        mixed = (
            stream
            + by_columns(att_m, out_m[:, :OUT_HALF])
            + by_columns(att_o, out_o[:, :OUT_HALF])
        )
        normed_two, scale_two = rms_forward(mixed, gain_twos[layer])
        normed_two = normed_two.astype(BF)
        normed_pair = jnp.concatenate([normed_two, swap(normed_two, "tp")], axis=0)
        hiddens = []
        kept = []
        for weight in (gu_m, gu_o):
            both = product(normed_pair, weight)
            gate, up_value = both[:, :hid], both[:, hid:]
            sigma = jax.nn.sigmoid(gate)
            hidden = (gate * sigma * up_value).astype(BF)
            hiddens.append(hidden)
            kept.append((gate, up_value, hidden))
        partial = by_columns(hiddens[0], down_m) + by_columns(hiddens[1], down_o)
        saved.append(
            (
                stream,
                scale_one,
                normed_one,
                query,
                key_value,
                log_totals,
                att_m,
                att_o,
                mixed,
                scale_two,
                normed_pair,
                kept,
            )
        )
        stream = mixed + partial[:rows] + swap(partial[rows:].astype(BF), "tp").astype(F32)
    block_out = cut_features(stream)

    grad_stream = pad_features(cotangent)
    results = [None] * layers
    for layer in reversed(range(layers)):
        qkv_m, out_m = att_mine[layer]
        qkv_o, out_o = att_other[layer]
        gu_m, down_m = ffn_mine[layer]
        gu_o, down_o = ffn_other[layer]
        (
            layer_input,
            scale_one,
            normed_one,
            query,
            key_value,
            log_totals,
            att_m,
            att_o,
            mixed,
            scale_two,
            normed_pair,
            kept,
        ) = saved[layer]
        grad_out_b = grad_stream.astype(BF)
        grad_pair = jnp.concatenate([grad_out_b, swap(grad_out_b, "tp")], axis=0)
        partial = 0.0
        ffn_grads = []
        for (gate, up_value, hidden), gu, down in (
            (kept[0], gu_m, down_m),
            (kept[1], gu_o, down_o),
        ):
            grad_hidden = product(grad_pair, down)
            sigma = jax.nn.sigmoid(gate)
            grad_up_in = (grad_hidden * gate * sigma).astype(BF)
            grad_gate_in = (
                grad_hidden * up_value * sigma * (1.0 + gate * (1.0 - sigma))
            ).astype(BF)
            grad_gu = jnp.concatenate([grad_gate_in, grad_up_in], axis=1)
            partial = partial + by_columns(grad_gu, gu)
            ffn_grads.append(diagonal([normed_pair, grad_pair], [grad_gu, hidden]))
        arrived = swap(partial[rows:].astype(BF), "tp")
        arrived, ffn_grads = lax.optimization_barrier((arrived, ffn_grads))
        if layer > 0:
            ffn_sum = core_sum(ffn_grads[0], ffn_grads[1])
        else:
            later_sum = merge_sum(att_pair, ffn_grads)
        grad_normed_two = partial[:rows] + arrived.astype(F32)
        grad_mixed_norm, gain_two_terms = rms_backward(
            mixed, scale_two, gain_twos[layer], grad_normed_two
        )
        grad_mixed = grad_stream + grad_mixed_norm
        grad_mixed_b = grad_mixed.astype(BF)
        grad_attended_b = join(
            product(grad_mixed_b, out_m)[:, :OUT_HALF], product(grad_mixed_b, out_o)[:, :OUT_HALF]
        ).astype(BF)
        if layer > 0:
            ffn_sum, grad_attended_b = lax.optimization_barrier((ffn_sum, grad_attended_b))
            ffn_done = scatter_plane(ffn_sum)
        else:
            later_sum, grad_attended_b, ffn_done = lax.optimization_barrier(
                (later_sum, grad_attended_b, ffn_done)
            )
            later = scatter_plane(later_sum)
        grad_query, key_value_terms = attention_back(
            query, key_value, grad_attended_b, log_totals, codes
        )
        key_value_grad = scatter_group(key_value_terms)
        grad_qkv = jnp.concatenate(
            [
                rotate(
                    jnp.concatenate([grad_query, key_value_grad[:, :KVW]], axis=1),
                    cosine,
                    sine,
                    -1.0,
                ),
                key_value_grad[:, KVW:],
            ],
            axis=1,
        ).astype(BF)
        grad_m, grad_o = halves(grad_qkv, QKV_HALF)
        wide = ((0, 0), (0, QKV_PAD - QKV_HALF))
        grad_m, grad_o = jnp.pad(grad_m, wide), jnp.pad(grad_o, wide)
        grad_normed_one = by_columns(grad_m, qkv_m) + by_columns(grad_o, qkv_o)
        grad_input_norm, gain_one_terms = rms_backward(
            layer_input, scale_one, gain_ones[layer], grad_normed_one
        )
        grad_stream = grad_mixed + grad_input_norm
        ones = jnp.ones((rows, OUT_PAD - OUT_HALF), BF)
        att_grads = [
            diagonal(
                [normed_one, gain_one_terms, grad_mixed_b, gain_two_terms],
                [
                    grad_part[:, :QKV_HALF],
                    jnp.ones((rows, QKV_PAD - QKV_HALF), BF),
                    att_part,
                    ones,
                ],
            )
            for grad_part, att_part in ((grad_m, att_m), (grad_o, att_o))
        ]
        if layer > 0:
            grad_stream, att_pair = lax.optimization_barrier((grad_stream, att_grads))
        else:
            ffn_one = low_sum(ffn_done)
            ffn_one = (ffn_one, swap(ffn_one, "core"))
            att_grads, ffn_one = lax.optimization_barrier((att_grads, ffn_one))
            att_zero = z_sum(plane_scatter(core_sum(att_grads[0], att_grads[1]), 768))
            att_one = z_sum(later[:, :ATT])
            ffn_zero = low_sum(later[:, ATT:])
            ffn_zero = (ffn_zero, swap(ffn_zero, "core"))

    query_grads, key_grads, value_grads, out_grads, gain_grads = write_grads(
        lax.axis_index("core").astype(jnp.int32).reshape(1),
        (att_zero, swap(att_zero, "core"), att_one, swap(att_one, "core")),
    )
    ffn_outs = [
        jnp.stack(
            [
                join(
                    mine[:PER, at * hid : (at + 1) * hid], other[:PER, at * hid : (at + 1) * hid]
                ).astype(F32)
                for mine, other in (ffn_zero, ffn_one)
            ]
        )
        for at in range(3)
    ]
    return (
        block_out,
        cut_features(grad_stream),
        gain_grads[:2, 0, :PER],
        query_grads,
        key_grads,
        value_grads,
        out_grads,
        gain_grads[2:, 0, :PER],
    ) + tuple(ffn_outs)


def solution(mesh):
    fine = Mesh(mesh.devices.reshape(Y, X, ZL, CORE, TP), ("y", "x", "zl", "core", "tp"))
    every = ("y", "x", "zl", "core", "tp")
    return jax.shard_map(
        shards,
        mesh=fine,
        in_specs=(
            P(every, None),
            P(every),
            P(every),
            P(every, None),
            P(None, XY),
            P(None, XY, None),
            P(None, XY, None),
            P(None, XY, None),
            P(None, XY, None),
            P(None, XY),
            P(None, XY, "tp"),
            P(None, XY, "tp"),
            P(None, XY, "tp"),
        ),
        out_specs=(
            P(every, None),
            P(every, None),
            P(None, XY),
            P(None, XY, None),
            P(None, XY, None),
            P(None, XY, None),
            P(None, XY, None),
            P(None, XY),
            P(None, XY, "tp"),
            P(None, XY, "tp"),
            P(None, XY, "tp"),
        ),
        check_vma=False,
    )
```

```python
import jax
import jax.numpy as jnp
from jax import lax
from jax.experimental import pallas as pl
from jax.experimental.pallas import tpu as pltpu
from jax.sharding import Mesh, PartitionSpec as P

D = 960
HEADS = 15
KV_HEADS = 5
HEAD = 64
QW = HEADS * HEAD
KVW = KV_HEADS * HEAD

EPSILON = 1e-05
THETA = 100000.0
MASKED = -1e30

Y, X, ZL, CORE, TP = 4, 4, 2, 2, 2
XY = ("y", "x")
PER = D // (Y * X)
PAD = 64
DP = PAD * Y * X
QKV_HALF = (QW + 2 * KVW) // 2
QKV_PAD = 896
OUT_HALF = QW // 2
OUT_PAD = 512
ATT = QKV_PAD + OUT_PAD
BF = jnp.bfloat16
VM = pl.BlockSpec(memory_space=pltpu.VMEM)
F32 = jnp.float32


def product(left, right):
    return jnp.dot(left, right, preferred_element_type=F32)


def by_rows(left, right):
    return lax.dot_general(left, right, (((0,), (0,)), ((), ())), preferred_element_type=F32)


def by_columns(left, right):
    return lax.dot_general(left, right, (((1,), (1,)), ((), ())), preferred_element_type=F32)


def ring(size, step):
    return [(i, (i + step) % size) for i in range(size)]


def z_ring(step):
    pairs = []
    for low in range(ZL):
        for high in range(TP):
            there = (high * ZL + low + step) % (ZL * TP)
            pairs.append((low * TP + high, (there % ZL) * TP + there // ZL))
    return pairs


def swap(values, axis):
    return lax.ppermute(values, axis, [(0, 1), (1, 0)])


def z_send(values, step):
    return lax.ppermute(values, ("zl", "tp"), z_ring(step))


STEPS = (2, 1, 3)


def gather_group(values):
    mine = jnp.concatenate([values] + [z_send(values, step) for step in STEPS], axis=0)
    return jnp.concatenate([mine, swap(mine, "core")], axis=0)


def scatter_group(terms):
    half = terms.shape[0] // 2
    rows = half // 4
    total = terms[:half].astype(F32) + swap(terms[half:].astype(BF), "core").astype(F32)
    out = total[:rows]
    for at, step in enumerate(STEPS):
        block = total[(at + 1) * rows : (at + 2) * rows].astype(BF)
        out = out + z_send(block, -step).astype(F32)
    return out


def line_scatter(values, axis):
    at = lax.axis_index(axis)
    out = lax.dynamic_index_in_dim(values, at, 0, False).astype(F32)
    for step in STEPS:
        block = lax.dynamic_index_in_dim(values, (at + step) % 4, 0, False)
        out = out + lax.ppermute(block, axis, ring(4, step)).astype(F32)
    return out


def plane_scatter(values, cut):
    view = values.reshape(Y, X, PAD, values.shape[1])
    first = line_scatter(jnp.swapaxes(view[..., :cut], 0, 1), "x").astype(BF)
    second = line_scatter(view[..., cut:], "y").astype(BF)
    first = line_scatter(first, "y")
    second = line_scatter(second, "x")
    return jnp.concatenate([first, second], axis=1)


def low_sum(part):
    part = part.astype(BF)
    return (part.astype(F32) + swap(part, "zl").astype(F32)).astype(BF)


def z_sum(part):
    part = part.astype(BF)
    two, one, three = (z_send(part, step).astype(F32) for step in STEPS)
    return ((part.astype(F32) + two) + (one + three)).astype(BF)


def grads_kernel(plan, *refs):
    out_ref = refs[-1]
    for at, start, stop in plan["dots"]:
        part = by_rows(refs[at][...], refs[at + 1][...])
        for low, high, extra in plan["spans"]:
            if extra is not None and low <= start and stop <= high:
                part = part + refs[extra][:, start - low : stop - low].astype(F32)
        out_ref[:, start:stop] = part.astype(BF)


def weight_grads(sections):
    operands, dots, spans, base = [], [], [], 0
    for pairs, extra in sections:
        start = base
        for left, right in pairs:
            dots.append((len(operands), base, base + right.shape[1]))
            operands += [left, right]
            base += right.shape[1]
        spans.append((start, base, None if extra is None else len(operands)))
        if extra is not None:
            operands.append(extra)
    plan = {"dots": dots, "spans": spans}

    def kernel(*refs):
        grads_kernel(plan, *refs)

    return pl.pallas_call(
        kernel,
        out_shape=jax.ShapeDtypeStruct((DP, base), BF),
        in_specs=[VM] * len(operands),
        out_specs=VM,
        compiler_params=pltpu.CompilerParams(vmem_limit_bytes=48 * 2**20),
        cost_estimate=pl.CostEstimate(
            flops=2 * DP * base * 640, bytes_accessed=4 * DP * base, transcendentals=0
        ),
        name="weight_grads",
    )(*operands)


def write_kernel(flag_ref, *refs):
    ins, outs, gain_ref, qkv_ref, out_ref = refs[:10], refs[10:17], *refs[17:]
    first = flag_ref[0] == 0
    shape = (8, OUT_PAD - OUT_HALF)
    chooser = (
        lax.broadcasted_iota(jnp.int32, shape, 0) == lax.broadcasted_iota(jnp.int32, shape, 1)
    ).astype(BF)
    hid = ins[4].shape[1] // 3

    def both(pair, start, width):
        mine, other = ins[pair][:, start : start + width], ins[pair + 1][:, start : start + width]
        low, high = jnp.where(first, mine, other), jnp.where(first, other, mine)
        return low.astype(F32), high.astype(F32)

    def gain(slot, pair, start):
        low = both(pair, start, OUT_PAD - OUT_HALF)[0]
        gain_ref[slot] = by_columns(chooser, low.astype(BF))

    for layer, (pair, start) in enumerate(((4, 0), (8, 0))):
        for at in range(3):
            low, high = both(pair, at * hid, hid)
            outs[4 + at][:, layer, :hid] = low[:PER]
            outs[4 + at][:, layer, hid:] = high[:PER]
    for layer, (pair, start) in enumerate(((2, QKV_PAD), (6, 0))):
        low, high = both(pair, start, OUT_HALF)
        out_ref[:, :OUT_HALF] = low
        out_ref[:, OUT_HALF:] = high
        outs[3][:, layer, :] = out_ref[:PER, :]
        gain(2 + layer, pair, start + OUT_HALF)
    for layer, pair in enumerate((0, 2)):
        low, high = both(pair, 0, QKV_HALF)
        qkv_ref[:, :QKV_HALF] = low
        qkv_ref[:, QKV_HALF:] = high
        outs[0][:, layer, :] = qkv_ref[:PER, :QW]
        outs[1][:, layer, :] = qkv_ref[:PER, QW : QW + KVW]
        outs[2][:, layer, :] = qkv_ref[:PER, QW + KVW :]
        gain(layer, pair, QKV_HALF)


def write_grads(flag, parts):
    hid = parts[4].shape[1] // 3
    shapes = [(PER, 2, width) for width in (QW, KVW, KVW, QW, 2 * hid, 2 * hid, 2 * hid)]
    outs = pl.pallas_call(
        write_kernel,
        out_shape=tuple(jax.ShapeDtypeStruct(shape, F32) for shape in shapes + [(4, 8, PAD)]),
        in_specs=[pl.BlockSpec(memory_space=pltpu.SMEM)] + [VM] * 10,
        out_specs=(VM,) * 8,
        scratch_shapes=[pltpu.VMEM((PAD, QW + 2 * KVW), F32), pltpu.VMEM((PAD, QW), F32)],
        compiler_params=pltpu.CompilerParams(vmem_limit_bytes=40 * 2**20),
        name="write_grads",
    )(flag, *parts)
    return [jnp.swapaxes(out, 0, 1) for out in outs[:7]] + [outs[7]]


def scatter_plane(total):
    return lax.psum_scatter(total, XY, scatter_dimension=0, tiled=True)


def rope_tables(positions):
    half_head = HEAD // 2
    freqs = THETA ** (-2.0 * jnp.arange(half_head, dtype=F32) / HEAD)
    angles = positions.astype(F32)[:, None] * freqs[None, :]
    return (jnp.cos(angles), jnp.sin(angles))


def rotate(values, cosine, sine, direction):
    row_count = values.shape[0]
    split_view = values.reshape(row_count, -1, 2, HEAD // 2)
    first_half = split_view[:, :, 0]
    second_half = split_view[:, :, 1]
    cos_rows = cosine[:, None, :]
    sin_rows = direction * sine[:, None, :]
    turned = jnp.stack(
        [
            first_half * cos_rows - second_half * sin_rows,
            second_half * cos_rows + first_half * sin_rows,
        ],
        axis=2,
    )
    return turned.reshape(row_count, -1)


def rms_forward(values, gain):
    mean = jnp.sum(values * values, axis=-1, keepdims=True) * (1.0 / D)
    scale = lax.rsqrt(mean + EPSILON)
    return (values * scale * gain, scale)


def rms_backward(values, scale, gain, grad_normed):
    weighted = grad_normed * gain
    mean = jnp.sum(weighted * values, axis=-1, keepdims=True) * (1.0 / D)
    grad_values = scale * weighted - values * (scale * scale * scale) * mean
    return (grad_values, (grad_normed * values * scale).astype(BF))


SHARE = HEADS // KV_HEADS


def head_stack(ref, group):
    return jnp.concatenate(
        [
            ref[:, (group * SHARE + at) * HEAD : (group * SHARE + at + 1) * HEAD]
            for at in range(SHARE)
        ],
        axis=0,
    )


def mask_bias(codes):
    segment_q, position_q, segment_k, position_k = codes
    seen = (segment_k[...] == segment_q[...]) & (position_k[...] <= position_q[...])
    return jnp.where(seen, 0.0, MASKED)


def attend_kernel(q_ref, kv_ref, sq, pq, sk, pk, att_ref, lse_ref, bias_ref):
    rows = q_ref.shape[0]
    bias_ref[...] = mask_bias((sq, pq, sk, pk))
    for group in range(KV_HEADS):
        query = head_stack(q_ref, group) * BF(HEAD ** (-0.5))
        key = kv_ref[:, group * HEAD : (group + 1) * HEAD]
        value = kv_ref[:, KVW + group * HEAD : KVW + (group + 1) * HEAD]
        scores = by_columns(key, query) + bias_ref[...]
        top = jnp.max(scores, axis=0, keepdims=True)
        terms = jnp.exp(scores - top)
        total = jnp.sum(terms, axis=0, keepdims=True)
        lse_ref[group : group + 1, :] = top + jnp.log(total)
        out = (by_rows(value, terms.astype(BF)) * (1.0 / total)).T
        for at in range(SHARE):
            head = group * SHARE + at
            att_ref[:, head * HEAD : (head + 1) * HEAD] = out[
                at * rows : (at + 1) * rows
            ].astype(BF)


def attend_back_kernel(
    q_ref, kv_ref, da_ref, lse_ref, sq, pq, sk, pk, dq_ref, dkv_ref, bias_ref
):
    rows = q_ref.shape[0]
    bias_ref[...] = mask_bias((sq, pq, sk, pk))
    for group in range(KV_HEADS):
        query = head_stack(q_ref, group) * BF(HEAD ** (-0.5))
        grad = head_stack(da_ref, group)
        key = kv_ref[:, group * HEAD : (group + 1) * HEAD]
        value = kv_ref[:, KVW + group * HEAD : KVW + (group + 1) * HEAD]
        probs = jnp.exp(by_columns(key, query) + bias_ref[...] - lse_ref[group : group + 1, :])
        grad_probs = by_columns(value, grad)
        delta = jnp.sum(probs * grad_probs, axis=0, keepdims=True)
        grad_scores = (probs * (grad_probs - delta)).astype(BF)
        dkv_ref[:, group * HEAD : (group + 1) * HEAD] = product(grad_scores, query).astype(BF)
        dkv_ref[:, KVW + group * HEAD : KVW + (group + 1) * HEAD] = product(
            probs.astype(BF), grad
        ).astype(BF)
        out = (by_rows(key, grad_scores) * (HEAD ** (-0.5))).T
        for at in range(SHARE):
            head = group * SHARE + at
            dq_ref[:, head * HEAD : (head + 1) * HEAD] = out[at * rows : (at + 1) * rows]


def attention(query, key_value, codes):
    rows, keys = query.shape[0], key_value.shape[0]
    return pl.pallas_call(
        attend_kernel,
        out_shape=(
            jax.ShapeDtypeStruct((rows, QW), BF),
            jax.ShapeDtypeStruct((8, SHARE * rows), F32),
        ),
        in_specs=[VM] * 6,
        out_specs=(VM, VM),
        scratch_shapes=[pltpu.VMEM((keys, SHARE * rows), F32)],
        compiler_params=pltpu.CompilerParams(vmem_limit_bytes=40 * 2**20),
        cost_estimate=pl.CostEstimate(
            flops=16 * HEADS * HEAD * rows * keys,
            bytes_accessed=4 * 2**20,
            transcendentals=HEADS * rows * keys,
        ),
        name="attend",
    )(query, key_value, *codes)


def attention_back(query, key_value, grad_attended_b, log_totals, codes):
    rows, keys = query.shape[0], key_value.shape[0]
    return pl.pallas_call(
        attend_back_kernel,
        out_shape=(
            jax.ShapeDtypeStruct((rows, QW), F32),
            jax.ShapeDtypeStruct((keys, 2 * KVW), BF),
        ),
        in_specs=[VM] * 8,
        out_specs=(VM, VM),
        scratch_shapes=[pltpu.VMEM((keys, SHARE * rows), F32)],
        compiler_params=pltpu.CompilerParams(vmem_limit_bytes=48 * 2**20),
        cost_estimate=pl.CostEstimate(
            flops=40 * HEADS * HEAD * rows * keys,
            bytes_accessed=6 * 2**20,
            transcendentals=HEADS * rows * keys,
        ),
        name="attend_back",
    )(query, key_value, grad_attended_b, log_totals, *codes)


def pad_features(values):
    rows = values.shape[0]
    view = values.reshape(rows, Y * X, PER)
    return jnp.pad(view, ((0, 0), (0, 0), (0, PAD - PER))).reshape(rows, DP)


def cut_features(values):
    rows = values.shape[0]
    return values.reshape(rows, Y * X, PAD)[:, :, :PER].reshape(rows, D)


def shards(
    tokens,
    segment_ids,
    positions,
    cotangent,
    attn_gain,
    w_query,
    w_key,
    w_value,
    w_out,
    ffn_gain,
    w_gate,
    w_up,
    w_down,
):
    layers = attn_gain.shape[0]
    rows = tokens.shape[0]
    hid = w_gate.shape[2] // 2
    first_core = lax.axis_index("core") == 0

    def pick(low, high):
        return jnp.where(first_core, low, high), jnp.where(first_core, high, low)

    def halves(whole, width):
        return pick(whole[..., :width], whole[..., width:])

    def join(mine, other):
        low, high = pick(mine, other)
        return jnp.concatenate([low, high], axis=-1)

    def tall(values):
        return jnp.pad(values, ((0, PAD - PER), (0, 0)))

    gain_columns = jnp.stack(
        [attn_gain[layer] for layer in range(layers)] + [ffn_gain[layer] for layer in range(layers)],
        axis=1,
    )
    gain_columns = jnp.pad(gain_columns, ((0, 0), (0, OUT_PAD - OUT_HALF - 2 * layers)))
    packs = []
    for layer in range(layers):
        qkv = jnp.concatenate([w_query[layer], w_key[layer], w_value[layer]], axis=1)
        qkv_mine = jnp.pad(halves(qkv, QKV_HALF)[0], ((0, 0), (0, QKV_PAD - QKV_HALF)))
        out_mine = halves(w_out[layer], OUT_HALF)[0]
        packs.append(jnp.concatenate([qkv_mine, out_mine, gain_columns], axis=1))
        packs.append(
            jnp.concatenate(
                [halves(w[layer], hid)[0] for w in (w_gate, w_up, w_down)], axis=1
            )
        )
    packs = [tall(pack) for pack in packs]
    att_mine, att_other, ffn_mine, ffn_other = [], [], [], []
    for layer in range(layers):
        whole = lax.all_gather(
            jnp.concatenate(packs[2 * layer : 2 * layer + 2], axis=1), XY, axis=0, tiled=True
        )
        att = whole[:, :ATT]
        ffn = whole[:, ATT:]
        for part, att_list, ffn_list in (
            ((att, ffn), att_mine, ffn_mine),
            ((swap(att, "core"), swap(ffn, "core")), att_other, ffn_other),
        ):
            att_list.append((part[0][:, :QKV_PAD], part[0][:, QKV_PAD:]))
            ffn_list.append((part[1][:, : 2 * hid], part[1][:, 2 * hid :]))

    chooser = jnp.eye(8, OUT_PAD - OUT_HALF, dtype=BF)
    gains = by_columns(chooser, att_mine[0][1][:, OUT_HALF:])
    gain_ones = [gains[layer : layer + 1] for layer in range(layers)]
    gain_twos = [gains[layers + layer : layers + layer + 1] for layer in range(layers)]

    cosine, sine = rope_tables(positions)
    stamps = gather_group(jnp.stack([segment_ids, positions], axis=1))
    codes = (
        jnp.tile(segment_ids, SHARE)[None, :],
        jnp.tile(positions, SHARE)[None, :],
        stamps[:, :1],
        stamps[:, 1:],
    )
    stream = pad_features(tokens)
    saved = []
    for layer in range(layers):
        qkv_m, out_m = att_mine[layer]
        qkv_o, out_o = att_other[layer]
        gu_m, down_m = ffn_mine[layer]
        gu_o, down_o = ffn_other[layer]
        normed_one, scale_one = rms_forward(stream, gain_ones[layer])
        normed_one = normed_one.astype(BF)
        qkv = join(
            product(normed_one, qkv_m)[:, :QKV_HALF], product(normed_one, qkv_o)[:, :QKV_HALF]
        )
        turned = rotate(qkv[:, : QW + KVW], cosine, sine, 1.0).astype(BF)
        query = turned[:, :QW]
        key_value = jnp.concatenate([turned[:, QW:], qkv[:, QW + KVW :].astype(BF)], axis=1)
        key_value = gather_group(key_value)
        attended, log_totals = attention(query, key_value, codes)
        att_m, att_o = halves(attended, OUT_HALF)
        mixed = (
            stream
            + by_columns(att_m, out_m[:, :OUT_HALF])
            + by_columns(att_o, out_o[:, :OUT_HALF])
        )
        normed_two, scale_two = rms_forward(mixed, gain_twos[layer])
        normed_two = normed_two.astype(BF)
        normed_pair = jnp.concatenate([normed_two, swap(normed_two, "tp")], axis=0)
        hiddens = []
        kept = []
        for weight in (gu_m, gu_o):
            both = product(normed_pair, weight)
            gate, up_value = both[:, :hid], both[:, hid:]
            sigma = jax.nn.sigmoid(gate)
            hidden = (gate * sigma * up_value).astype(BF)
            hiddens.append(hidden)
            kept.append((gate, up_value, hidden))
        partial = by_columns(hiddens[0], down_m) + by_columns(hiddens[1], down_o)
        saved.append(
            (
                stream,
                scale_one,
                normed_one,
                query,
                key_value,
                log_totals,
                att_m,
                att_o,
                mixed,
                scale_two,
                normed_pair,
                kept,
            )
        )
        stream = mixed + partial[:rows] + swap(partial[rows:].astype(BF), "tp").astype(F32)
    block_out = cut_features(stream)

    grad_stream = pad_features(cotangent)
    results = [None] * layers
    for layer in reversed(range(layers)):
        qkv_m, out_m = att_mine[layer]
        qkv_o, out_o = att_other[layer]
        gu_m, down_m = ffn_mine[layer]
        gu_o, down_o = ffn_other[layer]
        (
            layer_input,
            scale_one,
            normed_one,
            query,
            key_value,
            log_totals,
            att_m,
            att_o,
            mixed,
            scale_two,
            normed_pair,
            kept,
        ) = saved[layer]
        grad_out_b = grad_stream.astype(BF)
        grad_pair = jnp.concatenate([grad_out_b, swap(grad_out_b, "tp")], axis=0)
        partial = 0.0
        ffn_grads = []
        for (gate, up_value, hidden), gu, down in (
            (kept[0], gu_m, down_m),
            (kept[1], gu_o, down_o),
        ):
            grad_hidden = product(grad_pair, down)
            sigma = jax.nn.sigmoid(gate)
            grad_up_in = (grad_hidden * gate * sigma).astype(BF)
            grad_gate_in = (
                grad_hidden * up_value * sigma * (1.0 + gate * (1.0 - sigma))
            ).astype(BF)
            grad_gu = jnp.concatenate([grad_gate_in, grad_up_in], axis=1)
            partial = partial + by_columns(grad_gu, gu)
            ffn_grads.append([(normed_pair, grad_gu), (grad_pair, hidden)])
        arrived = swap(partial[rows:].astype(BF), "tp")
        ffn_give = weight_grads([(ffn_grads[1], None)])
        arrived, ffn_give = lax.optimization_barrier((arrived, ffn_give))
        ffn_got = swap(ffn_give, "core")
        grad_normed_two = partial[:rows] + arrived.astype(F32)
        grad_mixed_norm, gain_two_terms = rms_backward(
            mixed, scale_two, gain_twos[layer], grad_normed_two
        )
        grad_mixed = grad_stream + grad_mixed_norm
        grad_mixed_b = grad_mixed.astype(BF)
        grad_attended_b = join(
            product(grad_mixed_b, out_m)[:, :OUT_HALF], product(grad_mixed_b, out_o)[:, :OUT_HALF]
        ).astype(BF)
        ones = jnp.ones((rows, OUT_PAD - OUT_HALF), BF)
        out_pairs = [
            [(grad_mixed_b, att_part), (gain_two_terms, ones)] for att_part in (att_m, att_o)
        ]
        out_give = weight_grads([(out_pairs[1], None)])
        out_give, grad_attended_b = lax.optimization_barrier((out_give, grad_attended_b))
        out_got = swap(out_give, "core")
        grad_query, key_value_terms = attention_back(
            query, key_value, grad_attended_b, log_totals, codes
        )
        key_value_terms, out_got, ffn_got = lax.optimization_barrier(
            (key_value_terms, out_got, ffn_got)
        )
        sections = [(out_pairs[0], out_got), (ffn_grads[0], ffn_got)]
        if layer > 0:
            group_one = weight_grads(sections)
        else:
            group_two = weight_grads([(pairs_one[0], got_one)] + sections)
        key_value_grad = scatter_group(key_value_terms)
        if layer > 0:
            key_value_grad, group_one = lax.optimization_barrier((key_value_grad, group_one))
            done_one = scatter_plane(group_one)
        else:
            key_value_grad, group_two, done_one = lax.optimization_barrier(
                (key_value_grad, group_two, done_one)
            )
            done_two = scatter_plane(group_two)
        grad_qkv = jnp.concatenate(
            [
                rotate(
                    jnp.concatenate([grad_query, key_value_grad[:, :KVW]], axis=1),
                    cosine,
                    sine,
                    -1.0,
                ),
                key_value_grad[:, KVW:],
            ],
            axis=1,
        ).astype(BF)
        grad_m, grad_o = halves(grad_qkv, QKV_HALF)
        wide = ((0, 0), (0, QKV_PAD - QKV_HALF))
        grad_m, grad_o = jnp.pad(grad_m, wide), jnp.pad(grad_o, wide)
        grad_normed_one = by_columns(grad_m, qkv_m) + by_columns(grad_o, qkv_o)
        grad_input_norm, gain_one_terms = rms_backward(
            layer_input, scale_one, gain_ones[layer], grad_normed_one
        )
        grad_stream = grad_mixed + grad_input_norm
        wide_ones = jnp.ones((rows, QKV_PAD - QKV_HALF), BF)
        pairs = [
            [(normed_one, part[:, :QKV_HALF]), (gain_one_terms, wide_ones)]
            for part in (grad_m, grad_o)
        ]
        give = weight_grads([(pairs[1], None)])
        grad_stream, give = lax.optimization_barrier((grad_stream, give))
        got = swap(give, "core")
        if layer > 0:
            pairs_one, got_one = pairs, got

    out_one = z_sum(done_one[:, :OUT_PAD])
    ffn_one = low_sum(done_one[:, OUT_PAD:])
    total = weight_grads([(pairs[0], got)])
    total, out_one, ffn_one = lax.optimization_barrier((total, out_one, ffn_one))
    att_zero = z_sum(plane_scatter(total, 512))
    att_one = z_sum(done_two[:, :ATT])
    ffn_zero = low_sum(done_two[:, ATT:])
    parts = []
    for part in (att_zero, att_one, ffn_zero, out_one, ffn_one):
        parts += [part, swap(part, "core")]
    (
        query_grads,
        key_grads,
        value_grads,
        out_grads,
        gate_grads,
        up_grads,
        down_grads,
        gain_grads,
    ) = write_grads(lax.axis_index("core").astype(jnp.int32).reshape(1), parts)
    return (
        block_out,
        cut_features(grad_stream),
        gain_grads[:2, 0, :PER],
        query_grads,
        key_grads,
        value_grads,
        out_grads,
        gain_grads[2:, 0, :PER],
        gate_grads,
        up_grads,
        down_grads,
    )


def solution(mesh):
    fine = Mesh(mesh.devices.reshape(Y, X, ZL, CORE, TP), ("y", "x", "zl", "core", "tp"))
    every = ("y", "x", "zl", "core", "tp")
    return jax.shard_map(
        shards,
        mesh=fine,
        in_specs=(
            P(every, None),
            P(every),
            P(every),
            P(every, None),
            P(None, XY),
            P(None, XY, None),
            P(None, XY, None),
            P(None, XY, None),
            P(None, XY, None),
            P(None, XY),
            P(None, XY, "tp"),
            P(None, XY, "tp"),
            P(None, XY, "tp"),
        ),
        out_specs=(
            P(every, None),
            P(every, None),
            P(None, XY),
            P(None, XY, None),
            P(None, XY, None),
            P(None, XY, None),
            P(None, XY, None),
            P(None, XY),
            P(None, XY, "tp"),
            P(None, XY, "tp"),
            P(None, XY, "tp"),
        ),
        check_vma=False,
    )
```

```python
import jax
import jax.numpy as jnp
from jax import lax
from jax.experimental import pallas as pl
from jax.experimental.pallas import tpu as pltpu
from jax.sharding import Mesh, PartitionSpec as P

D = 960
HEADS = 15
KV_HEADS = 5
HEAD = 64
QW = HEADS * HEAD
KVW = KV_HEADS * HEAD

EPSILON = 1e-05
THETA = 100000.0
MASKED = -1e30

Y, X, ZL, CORE, TP = 4, 4, 2, 2, 2
XY = ("y", "x")
PER = D // (Y * X)
PAD = 64
DP = PAD * Y * X
QKV_HALF = (QW + 2 * KVW) // 2
QKV_PAD = 896
OUT_HALF = QW // 2
OUT_PAD = 512
ATT = QKV_PAD + OUT_PAD
BF = jnp.bfloat16
VM = pl.BlockSpec(memory_space=pltpu.VMEM)
F32 = jnp.float32


def product(left, right):
    return jnp.dot(left, right, preferred_element_type=F32)


def by_rows(left, right):
    return lax.dot_general(left, right, (((0,), (0,)), ((), ())), preferred_element_type=F32)


def by_columns(left, right):
    return lax.dot_general(left, right, (((1,), (1,)), ((), ())), preferred_element_type=F32)


def ring(size, step):
    return [(i, (i + step) % size) for i in range(size)]


def z_ring(step):
    pairs = []
    for low in range(ZL):
        for high in range(TP):
            there = (high * ZL + low + step) % (ZL * TP)
            pairs.append((low * TP + high, (there % ZL) * TP + there // ZL))
    return pairs


def swap(values, axis):
    return lax.ppermute(values, axis, [(0, 1), (1, 0)])


def z_send(values, step):
    return lax.ppermute(values, ("zl", "tp"), z_ring(step))


STEPS = (2, 1, 3)


def gather_group(values):
    mine = jnp.concatenate([values] + [z_send(values, step) for step in STEPS], axis=0)
    return jnp.concatenate([mine, swap(mine, "core")], axis=0)


def scatter_group(terms):
    half = terms.shape[0] // 2
    rows = half // 4
    total = terms[:half].astype(F32) + swap(terms[half:].astype(BF), "core").astype(F32)
    out = total[:rows]
    for at, step in enumerate(STEPS):
        block = total[(at + 1) * rows : (at + 2) * rows].astype(BF)
        out = out + z_send(block, -step).astype(F32)
    return out


def line_scatter(values, axis):
    at = lax.axis_index(axis)
    out = lax.dynamic_index_in_dim(values, at, 0, False).astype(F32)
    for step in STEPS:
        block = lax.dynamic_index_in_dim(values, (at + step) % 4, 0, False)
        out = out + lax.ppermute(block, axis, ring(4, step)).astype(F32)
    return out


def plane_scatter(values, cut, others):
    view = values.reshape(Y, X, PAD, values.shape[1])
    first = line_scatter(jnp.swapaxes(view[..., :cut], 0, 1), "x").astype(BF)
    second = line_scatter(view[..., cut:], "y").astype(BF)
    first, second, others = lax.optimization_barrier((first, second, others))
    first = line_scatter(first, "y")
    second = line_scatter(second, "x")
    return (jnp.concatenate([first, second], axis=1),) + others


def low_sum(part):
    part = part.astype(BF)
    return (part.astype(F32) + swap(part, "zl").astype(F32)).astype(BF)


def z_sum(part):
    part = part.astype(BF)
    two, one, three = (z_send(part, step).astype(F32) for step in STEPS)
    return ((part.astype(F32) + two) + (one + three)).astype(BF)


def weight_grads(sections):
    operands, spans, base = [], [], 0
    for section in sections:
        width = section[1].shape[1]
        spans.append((len(operands), base, base + width))
        operands += list(section)
        base += width

    def kernel(*refs):
        for at, start, stop in spans:
            left, right, far_left, far_right = refs[at : at + 4]
            part = by_rows(left[...], right[...]) + by_rows(far_left[...], far_right[...])
            refs[-1][:, start:stop] = part.astype(BF)

    return pl.pallas_call(
        kernel,
        out_shape=jax.ShapeDtypeStruct((DP, base), BF),
        in_specs=[VM] * len(operands),
        out_specs=VM,
        compiler_params=pltpu.CompilerParams(vmem_limit_bytes=48 * 2**20),
        cost_estimate=pl.CostEstimate(
            flops=2 * DP * base * 640, bytes_accessed=4 * DP * base, transcendentals=0
        ),
        name="weight_grads",
    )(*operands)


def write_kernel(flag_ref, *refs):
    ins, outs, gain_ref, qkv_ref, out_ref = refs[:8], refs[8:15], *refs[15:]
    first = flag_ref[0] == 0
    shape = (8, OUT_PAD - OUT_HALF)
    chooser = (
        lax.broadcasted_iota(jnp.int32, shape, 0) == lax.broadcasted_iota(jnp.int32, shape, 1)
    ).astype(BF)
    hid = ins[4].shape[1] // 3

    def both(pair, start, width):
        mine, other = ins[pair][:, start : start + width], ins[pair + 1][:, start : start + width]
        low, high = jnp.where(first, mine, other), jnp.where(first, other, mine)
        return low.astype(F32), high.astype(F32)

    def gain(slot, pair, start):
        low = both(pair, start, OUT_PAD - OUT_HALF)[0]
        gain_ref[slot] = by_columns(chooser, low.astype(BF))

    for layer, (pair, start) in enumerate(((4, 0), (6, 0))):
        for at in range(3):
            low, high = both(pair, at * hid, hid)
            outs[4 + at][:, layer, :hid] = low[:PER]
            outs[4 + at][:, layer, hid:] = high[:PER]
    for layer, (pair, start) in enumerate(((0, QKV_PAD), (2, QKV_PAD))):
        low, high = both(pair, start, OUT_HALF)
        out_ref[:, :OUT_HALF] = low
        out_ref[:, OUT_HALF:] = high
        outs[3][:, layer, :] = out_ref[:PER, :]
        gain(2 + layer, pair, start + OUT_HALF)
    for layer, pair in enumerate((0, 2)):
        low, high = both(pair, 0, QKV_HALF)
        qkv_ref[:, :QKV_HALF] = low
        qkv_ref[:, QKV_HALF:] = high
        outs[0][:, layer, :] = qkv_ref[:PER, :QW]
        outs[1][:, layer, :] = qkv_ref[:PER, QW : QW + KVW]
        outs[2][:, layer, :] = qkv_ref[:PER, QW + KVW :]
        gain(layer, pair, QKV_HALF)


def write_grads(flag, parts):
    hid = parts[4].shape[1] // 3
    shapes = [(PER, 2, width) for width in (QW, KVW, KVW, QW, 2 * hid, 2 * hid, 2 * hid)]
    outs = pl.pallas_call(
        write_kernel,
        out_shape=tuple(jax.ShapeDtypeStruct(shape, F32) for shape in shapes + [(4, 8, PAD)]),
        in_specs=[pl.BlockSpec(memory_space=pltpu.SMEM)] + [VM] * 8,
        out_specs=(VM,) * 8,
        scratch_shapes=[pltpu.VMEM((PAD, QW + 2 * KVW), F32), pltpu.VMEM((PAD, QW), F32)],
        compiler_params=pltpu.CompilerParams(vmem_limit_bytes=40 * 2**20),
        name="write_grads",
    )(flag, *parts)
    return [jnp.swapaxes(out, 0, 1) for out in outs[:7]] + [outs[7]]


def scatter_plane(total):
    return lax.psum_scatter(total, XY, scatter_dimension=0, tiled=True)


def rope_tables(positions):
    half_head = HEAD // 2
    freqs = THETA ** (-2.0 * jnp.arange(half_head, dtype=F32) / HEAD)
    angles = positions.astype(F32)[:, None] * freqs[None, :]
    return (jnp.cos(angles), jnp.sin(angles))


def rotate(values, cosine, sine, direction):
    row_count = values.shape[0]
    split_view = values.reshape(row_count, -1, 2, HEAD // 2)
    first_half = split_view[:, :, 0]
    second_half = split_view[:, :, 1]
    cos_rows = cosine[:, None, :]
    sin_rows = direction * sine[:, None, :]
    turned = jnp.stack(
        [
            first_half * cos_rows - second_half * sin_rows,
            second_half * cos_rows + first_half * sin_rows,
        ],
        axis=2,
    )
    return turned.reshape(row_count, -1)


def rms_forward(values, gain):
    mean = jnp.sum(values * values, axis=-1, keepdims=True) * (1.0 / D)
    scale = lax.rsqrt(mean + EPSILON)
    return (values * scale * gain, scale)


def rms_backward(values, scale, gain, grad_normed):
    weighted = grad_normed * gain
    mean = jnp.sum(weighted * values, axis=-1, keepdims=True) * (1.0 / D)
    grad_values = scale * weighted - values * (scale * scale * scale) * mean
    return (grad_values, (grad_normed * values * scale).astype(BF))


SHARE = HEADS // KV_HEADS


def head_stack(ref, group):
    return jnp.concatenate(
        [
            ref[:, (group * SHARE + at) * HEAD : (group * SHARE + at + 1) * HEAD]
            for at in range(SHARE)
        ],
        axis=0,
    )


def mask_bias(codes):
    segment_q, position_q, segment_k, position_k = codes
    seen = (segment_k[...] == segment_q[...]) & (position_k[...] <= position_q[...])
    return jnp.where(seen, 0.0, MASKED)


def attend_kernel(q_ref, kv_ref, sq, pq, sk, pk, att_ref, lse_ref, bias_ref):
    rows = q_ref.shape[0]
    bias_ref[...] = mask_bias((sq, pq, sk, pk))
    for group in range(KV_HEADS):
        query = head_stack(q_ref, group) * BF(HEAD ** (-0.5))
        key = kv_ref[:, group * HEAD : (group + 1) * HEAD]
        value = kv_ref[:, KVW + group * HEAD : KVW + (group + 1) * HEAD]
        scores = by_columns(key, query) + bias_ref[...]
        top = jnp.max(scores, axis=0, keepdims=True)
        terms = jnp.exp(scores - top)
        total = jnp.sum(terms, axis=0, keepdims=True)
        lse_ref[group : group + 1, :] = top + jnp.log(total)
        out = (by_rows(value, terms.astype(BF)) * (1.0 / total)).T
        for at in range(SHARE):
            head = group * SHARE + at
            att_ref[:, head * HEAD : (head + 1) * HEAD] = out[
                at * rows : (at + 1) * rows
            ].astype(BF)


def attend_back_kernel(
    q_ref, kv_ref, da_ref, lse_ref, sq, pq, sk, pk, dq_ref, dkv_ref, bias_ref
):
    rows = q_ref.shape[0]
    bias_ref[...] = mask_bias((sq, pq, sk, pk))
    for group in range(KV_HEADS):
        query = head_stack(q_ref, group) * BF(HEAD ** (-0.5))
        grad = head_stack(da_ref, group)
        key = kv_ref[:, group * HEAD : (group + 1) * HEAD]
        value = kv_ref[:, KVW + group * HEAD : KVW + (group + 1) * HEAD]
        probs = jnp.exp(by_columns(key, query) + bias_ref[...] - lse_ref[group : group + 1, :])
        grad_probs = by_columns(value, grad)
        delta = jnp.sum(probs * grad_probs, axis=0, keepdims=True)
        grad_scores = (probs * (grad_probs - delta)).astype(BF)
        dkv_ref[:, group * HEAD : (group + 1) * HEAD] = product(grad_scores, query).astype(BF)
        dkv_ref[:, KVW + group * HEAD : KVW + (group + 1) * HEAD] = product(
            probs.astype(BF), grad
        ).astype(BF)
        out = (by_rows(key, grad_scores) * (HEAD ** (-0.5))).T
        for at in range(SHARE):
            head = group * SHARE + at
            dq_ref[:, head * HEAD : (head + 1) * HEAD] = out[at * rows : (at + 1) * rows]


def attention(query, key_value, codes):
    rows, keys = query.shape[0], key_value.shape[0]
    return pl.pallas_call(
        attend_kernel,
        out_shape=(
            jax.ShapeDtypeStruct((rows, QW), BF),
            jax.ShapeDtypeStruct((8, SHARE * rows), F32),
        ),
        in_specs=[VM] * 6,
        out_specs=(VM, VM),
        scratch_shapes=[pltpu.VMEM((keys, SHARE * rows), F32)],
        compiler_params=pltpu.CompilerParams(vmem_limit_bytes=40 * 2**20),
        cost_estimate=pl.CostEstimate(
            flops=16 * HEADS * HEAD * rows * keys,
            bytes_accessed=4 * 2**20,
            transcendentals=HEADS * rows * keys,
        ),
        name="attend",
    )(query, key_value, *codes)


def attention_back(query, key_value, grad_attended_b, log_totals, codes):
    rows, keys = query.shape[0], key_value.shape[0]
    return pl.pallas_call(
        attend_back_kernel,
        out_shape=(
            jax.ShapeDtypeStruct((rows, QW), F32),
            jax.ShapeDtypeStruct((keys, 2 * KVW), BF),
        ),
        in_specs=[VM] * 8,
        out_specs=(VM, VM),
        scratch_shapes=[pltpu.VMEM((keys, SHARE * rows), F32)],
        compiler_params=pltpu.CompilerParams(vmem_limit_bytes=48 * 2**20),
        cost_estimate=pl.CostEstimate(
            flops=40 * HEADS * HEAD * rows * keys,
            bytes_accessed=6 * 2**20,
            transcendentals=HEADS * rows * keys,
        ),
        name="attend_back",
    )(query, key_value, grad_attended_b, log_totals, *codes)


def pad_features(values):
    rows = values.shape[0]
    view = values.reshape(rows, Y * X, PER)
    return jnp.pad(view, ((0, 0), (0, 0), (0, PAD - PER))).reshape(rows, DP)


def cut_features(values):
    rows = values.shape[0]
    return values.reshape(rows, Y * X, PAD)[:, :, :PER].reshape(rows, D)


def shards(
    tokens,
    segment_ids,
    positions,
    cotangent,
    attn_gain,
    w_query,
    w_key,
    w_value,
    w_out,
    ffn_gain,
    w_gate,
    w_up,
    w_down,
):
    layers = attn_gain.shape[0]
    rows = tokens.shape[0]
    hid = w_gate.shape[2] // 2
    first_core = lax.axis_index("core") == 0

    def pick(low, high):
        return jnp.where(first_core, low, high), jnp.where(first_core, high, low)

    def halves(whole, width):
        return pick(whole[..., :width], whole[..., width:])

    def join(mine, other):
        low, high = pick(mine, other)
        return jnp.concatenate([low, high], axis=-1)

    def tall(values):
        return jnp.pad(values, ((0, PAD - PER), (0, 0)))

    gain_columns = jnp.stack(
        [attn_gain[layer] for layer in range(layers)] + [ffn_gain[layer] for layer in range(layers)],
        axis=1,
    )
    gain_columns = jnp.pad(gain_columns, ((0, 0), (0, OUT_PAD - OUT_HALF - 2 * layers)))
    packs = []
    for layer in range(layers):
        qkv = jnp.concatenate([w_query[layer], w_key[layer], w_value[layer]], axis=1)
        qkv_mine = jnp.pad(halves(qkv, QKV_HALF)[0], ((0, 0), (0, QKV_PAD - QKV_HALF)))
        out_mine = halves(w_out[layer], OUT_HALF)[0]
        packs.append(jnp.concatenate([qkv_mine, out_mine, gain_columns], axis=1))
        packs.append(
            jnp.concatenate(
                [halves(w[layer], hid)[0] for w in (w_gate, w_up, w_down)], axis=1
            )
        )
    packs = [tall(pack) for pack in packs]
    att_mine, att_other, ffn_mine, ffn_other = [], [], [], []
    for layer in range(layers):
        whole = lax.all_gather(
            jnp.concatenate(packs[2 * layer : 2 * layer + 2], axis=1), XY, axis=0, tiled=True
        )
        att = whole[:, :ATT]
        ffn = whole[:, ATT:]
        for part, att_list, ffn_list in (
            ((att, ffn), att_mine, ffn_mine),
            ((swap(att, "core"), swap(ffn, "core")), att_other, ffn_other),
        ):
            att_list.append((part[0][:, :QKV_PAD], part[0][:, QKV_PAD:]))
            ffn_list.append((part[1][:, : 2 * hid], part[1][:, 2 * hid :]))

    chooser = jnp.eye(8, OUT_PAD - OUT_HALF, dtype=BF)
    gains = by_columns(chooser, att_mine[0][1][:, OUT_HALF:])
    gain_ones = [gains[layer : layer + 1] for layer in range(layers)]
    gain_twos = [gains[layers + layer : layers + layer + 1] for layer in range(layers)]

    cosine, sine = rope_tables(positions)
    stamps = gather_group(jnp.stack([segment_ids, positions], axis=1))
    codes = (
        jnp.tile(segment_ids, SHARE)[None, :],
        jnp.tile(positions, SHARE)[None, :],
        stamps[:, :1],
        stamps[:, 1:],
    )
    stream = pad_features(tokens)
    saved = []
    for layer in range(layers):
        qkv_m, out_m = att_mine[layer]
        qkv_o, out_o = att_other[layer]
        gu_m, down_m = ffn_mine[layer]
        gu_o, down_o = ffn_other[layer]
        normed_one, scale_one = rms_forward(stream, gain_ones[layer])
        normed_one = normed_one.astype(BF)
        qkv = join(
            product(normed_one, qkv_m)[:, :QKV_HALF], product(normed_one, qkv_o)[:, :QKV_HALF]
        )
        turned = rotate(qkv[:, : QW + KVW], cosine, sine, 1.0).astype(BF)
        query = turned[:, :QW]
        key_value = jnp.concatenate([turned[:, QW:], qkv[:, QW + KVW :].astype(BF)], axis=1)
        key_value = gather_group(key_value)
        attended, log_totals = attention(query, key_value, codes)
        att_m, att_o = halves(attended, OUT_HALF)
        mixed = (
            stream
            + by_columns(att_m, out_m[:, :OUT_HALF])
            + by_columns(att_o, out_o[:, :OUT_HALF])
        )
        normed_two, scale_two = rms_forward(mixed, gain_twos[layer])
        normed_two = normed_two.astype(BF)
        normed_pair = jnp.concatenate([normed_two, swap(normed_two, "tp")], axis=0)
        hiddens = []
        kept = []
        for weight in (gu_m, gu_o):
            both = product(normed_pair, weight)
            gate, up_value = both[:, :hid], both[:, hid:]
            sigma = jax.nn.sigmoid(gate)
            hidden = (gate * sigma * up_value).astype(BF)
            hiddens.append(hidden)
            kept.append((gate, up_value, hidden))
        partial = by_columns(hiddens[0], down_m) + by_columns(hiddens[1], down_o)
        saved.append(
            (
                stream,
                scale_one,
                normed_one,
                query,
                key_value,
                log_totals,
                att_m,
                mixed,
                scale_two,
                normed_pair,
                kept,
                (
                    swap(normed_one, "core"),
                    swap(att_o, "core"),
                    swap(normed_pair, "core"),
                    swap(hiddens[1], "core"),
                ),
            )
        )
        stream = mixed + partial[:rows] + swap(partial[rows:].astype(BF), "tp").astype(F32)

    grad_stream = pad_features(cotangent)
    results = [None] * layers
    for layer in reversed(range(layers)):
        qkv_m, out_m = att_mine[layer]
        qkv_o, out_o = att_other[layer]
        gu_m, down_m = ffn_mine[layer]
        gu_o, down_o = ffn_other[layer]
        (
            layer_input,
            scale_one,
            normed_one,
            query,
            key_value,
            log_totals,
            att_m,
            mixed,
            scale_two,
            normed_pair,
            kept,
            (far_one, far_att, far_pair, far_hidden),
        ) = saved[layer]
        grad_out_b = grad_stream.astype(BF)
        grad_pair = jnp.concatenate([grad_out_b, swap(grad_out_b, "tp")], axis=0)
        far_grad_pair = swap(grad_pair, "core")
        partial = 0.0
        ffn_grads = []
        for (gate, up_value, hidden), gu, down in (
            (kept[0], gu_m, down_m),
            (kept[1], gu_o, down_o),
        ):
            grad_hidden = product(grad_pair, down)
            sigma = jax.nn.sigmoid(gate)
            grad_up_in = (grad_hidden * gate * sigma).astype(BF)
            grad_gate_in = (
                grad_hidden * up_value * sigma * (1.0 + gate * (1.0 - sigma))
            ).astype(BF)
            grad_gu = jnp.concatenate([grad_gate_in, grad_up_in], axis=1)
            partial = partial + by_columns(grad_gu, gu)
            ffn_grads.append(grad_gu)
        arrived = swap(partial[rows:].astype(BF), "tp")
        ffn_sections = [
            (normed_pair, ffn_grads[0], far_pair, swap(ffn_grads[1], "core")),
            (grad_pair, kept[0][2], far_grad_pair, far_hidden),
        ]
        if layer > 0:
            group_one = weight_grads(ffn_sections)
            arrived, group_one = lax.optimization_barrier((arrived, group_one))
            done_one = scatter_plane(group_one)
        else:
            group_two = weight_grads(att_sections + ffn_sections)
            arrived, group_two, done_one = lax.optimization_barrier(
                (arrived, group_two, done_one)
            )
            done_two = scatter_plane(group_two)
        grad_normed_two = partial[:rows] + arrived.astype(F32)
        grad_mixed_norm, gain_two_terms = rms_backward(
            mixed, scale_two, gain_twos[layer], grad_normed_two
        )
        grad_mixed = grad_stream + grad_mixed_norm
        grad_mixed_b = grad_mixed.astype(BF)
        grad_attended_b = join(
            product(grad_mixed_b, out_m)[:, :OUT_HALF], product(grad_mixed_b, out_o)[:, :OUT_HALF]
        ).astype(BF)
        far_mixed = swap(jnp.concatenate([grad_mixed_b, gain_two_terms], axis=0), "core")
        grad_query, key_value_terms = attention_back(
            query, key_value, grad_attended_b, log_totals, codes
        )
        key_value_grad = scatter_group(key_value_terms)
        grad_qkv = jnp.concatenate(
            [
                rotate(
                    jnp.concatenate([grad_query, key_value_grad[:, :KVW]], axis=1),
                    cosine,
                    sine,
                    -1.0,
                ),
                key_value_grad[:, KVW:],
            ],
            axis=1,
        ).astype(BF)
        grad_m, grad_o = halves(grad_qkv, QKV_HALF)
        wide = ((0, 0), (0, QKV_PAD - QKV_HALF))
        grad_m, grad_o = jnp.pad(grad_m, wide), jnp.pad(grad_o, wide)
        grad_normed_one = by_columns(grad_m, qkv_m) + by_columns(grad_o, qkv_o)
        grad_input_norm, gain_one_terms = rms_backward(
            layer_input, scale_one, gain_ones[layer], grad_normed_one
        )
        grad_stream = grad_mixed + grad_input_norm
        wide_ones = jnp.ones((rows, QKV_PAD - QKV_HALF), BF)
        ones = jnp.ones((rows, OUT_PAD - OUT_HALF), BF)
        far_qkv = swap(grad_o[:, :QKV_HALF], "core")
        att_sections = [
            (normed_one, grad_m[:, :QKV_HALF], far_one, far_qkv),
            (gain_one_terms, wide_ones, swap(gain_one_terms, "core"), wide_ones),
            (grad_mixed_b, att_m, far_mixed[:rows], far_att),
            (gain_two_terms, ones, far_mixed[rows:], ones),
        ]

    ffn_one = low_sum(done_one)
    total = weight_grads(att_sections)
    total, ffn_one = lax.optimization_barrier((total, ffn_one))
    total, block_out, input_grad = plane_scatter(
        total, 768, (cut_features(stream), cut_features(grad_stream))
    )
    att_zero = z_sum(total)
    att_one = z_sum(done_two[:, :ATT])
    ffn_zero = low_sum(done_two[:, ATT:])
    parts = []
    for part in (att_zero, att_one, ffn_zero, ffn_one):
        parts += [part, swap(part, "core")]
    (
        query_grads,
        key_grads,
        value_grads,
        out_grads,
        gate_grads,
        up_grads,
        down_grads,
        gain_grads,
    ) = write_grads(lax.axis_index("core").astype(jnp.int32).reshape(1), parts)
    return (
        block_out,
        input_grad,
        gain_grads[:2, 0, :PER],
        query_grads,
        key_grads,
        value_grads,
        out_grads,
        gain_grads[2:, 0, :PER],
        gate_grads,
        up_grads,
        down_grads,
    )


def solution(mesh):
    fine = Mesh(mesh.devices.reshape(Y, X, ZL, CORE, TP), ("y", "x", "zl", "core", "tp"))
    every = ("y", "x", "zl", "core", "tp")
    return jax.shard_map(
        shards,
        mesh=fine,
        in_specs=(
            P(every, None),
            P(every),
            P(every),
            P(every, None),
            P(None, XY),
            P(None, XY, None),
            P(None, XY, None),
            P(None, XY, None),
            P(None, XY, None),
            P(None, XY),
            P(None, XY, "tp"),
            P(None, XY, "tp"),
            P(None, XY, "tp"),
        ),
        out_specs=(
            P(every, None),
            P(every, None),
            P(None, XY),
            P(None, XY, None),
            P(None, XY, None),
            P(None, XY, None),
            P(None, XY, None),
            P(None, XY),
            P(None, XY, "tp"),
            P(None, XY, "tp"),
            P(None, XY, "tp"),
        ),
        check_vma=False,
    )
```

```python
import jax
import jax.numpy as jnp
from jax import lax
from jax.experimental import pallas as pl
from jax.experimental.pallas import tpu as pltpu
from jax.sharding import Mesh, PartitionSpec as P

D = 960
HEADS = 15
KV_HEADS = 5
HEAD = 64
QW = HEADS * HEAD
KVW = KV_HEADS * HEAD

EPSILON = 1e-05
THETA = 100000.0
MASKED = -1e30

Y, X, ZL, CORE, TP = 4, 4, 2, 2, 2
XY = ("y", "x")
PER = D // (Y * X)
PAD = 64
DP = PAD * Y * X
QKV_HALF = (QW + 2 * KVW) // 2
QKV_PAD = 896
OUT_HALF = QW // 2
OUT_PAD = 512
ATT = QKV_PAD + OUT_PAD
BF = jnp.bfloat16
VM = pl.BlockSpec(memory_space=pltpu.VMEM)
F32 = jnp.float32


def product(left, right):
    return jnp.dot(left, right, preferred_element_type=F32)


def by_rows(left, right):
    return lax.dot_general(left, right, (((0,), (0,)), ((), ())), preferred_element_type=F32)


def by_columns(left, right):
    return lax.dot_general(left, right, (((1,), (1,)), ((), ())), preferred_element_type=F32)


def ring(size, step):
    return [(i, (i + step) % size) for i in range(size)]


def z_ring(step):
    pairs = []
    for low in range(ZL):
        for high in range(TP):
            there = (high * ZL + low + step) % (ZL * TP)
            pairs.append((low * TP + high, (there % ZL) * TP + there // ZL))
    return pairs


def swap(values, axis):
    return lax.ppermute(values, axis, [(0, 1), (1, 0)])


def z_send(values, step):
    return lax.ppermute(values, ("zl", "tp"), z_ring(step))


STEPS = (2, 1, 3)


def gather_group(values):
    mine = jnp.concatenate([values] + [z_send(values, step) for step in STEPS], axis=0)
    return mine, swap(mine, "core")


def scatter_group(mine, other):
    rows = mine.shape[0] // 4
    total = mine + swap(other, "core").astype(F32)
    out = total[:rows]
    for at, step in enumerate(STEPS):
        block = total[(at + 1) * rows : (at + 2) * rows].astype(BF)
        out = out + z_send(block, -step).astype(F32)
    return out


def line_scatter(values, axis):
    at = lax.axis_index(axis)
    out = lax.dynamic_index_in_dim(values, at, 0, False).astype(F32)
    for step in STEPS:
        block = lax.dynamic_index_in_dim(values, (at + step) % 4, 0, False)
        out = out + lax.ppermute(block, axis, ring(4, step)).astype(F32)
    return out


def plane_scatter(values, cut, others):
    view = values.reshape(Y, X, PAD, values.shape[1])
    first = line_scatter(jnp.swapaxes(view[..., :cut], 0, 1), "x").astype(BF)
    second = line_scatter(view[..., cut:], "y").astype(BF)
    first, second, others = lax.optimization_barrier((first, second, others))
    first = line_scatter(first, "y")
    second = line_scatter(second, "x")
    return (jnp.concatenate([first, second], axis=1),) + others


def low_sum(part):
    part = part.astype(BF)
    return (part.astype(F32) + swap(part, "zl").astype(F32)).astype(BF)


def z_sum(part):
    part = part.astype(BF)
    two, one, three = (z_send(part, step).astype(F32) for step in STEPS)
    return ((part.astype(F32) + two) + (one + three)).astype(BF)


def weight_grads(sections):
    operands, spans, base = [], [], 0
    for section in sections:
        width = section[1].shape[1]
        spans.append((len(operands), base, base + width))
        operands += list(section)
        base += width

    def kernel(*refs):
        for at, start, stop in spans:
            left, right, far_left, far_right = refs[at : at + 4]
            part = by_rows(left[...], right[...]) + by_rows(far_left[...], far_right[...])
            refs[-1][:, start:stop] = part.astype(BF)

    return pl.pallas_call(
        kernel,
        out_shape=jax.ShapeDtypeStruct((DP, base), BF),
        in_specs=[VM] * len(operands),
        out_specs=VM,
        compiler_params=pltpu.CompilerParams(vmem_limit_bytes=48 * 2**20),
        cost_estimate=pl.CostEstimate(
            flops=2 * DP * base * 640, bytes_accessed=4 * DP * base, transcendentals=0
        ),
        name="weight_grads",
    )(*operands)


def write_kernel(flag_ref, *refs):
    ins, outs, gain_ref, qkv_ref, out_ref = refs[:8], refs[8:15], *refs[15:]
    first = flag_ref[0] == 0
    shape = (8, OUT_PAD - OUT_HALF)
    chooser = (
        lax.broadcasted_iota(jnp.int32, shape, 0) == lax.broadcasted_iota(jnp.int32, shape, 1)
    ).astype(BF)
    hid = ins[4].shape[1] // 3

    def both(pair, start, width):
        mine, other = ins[pair][:, start : start + width], ins[pair + 1][:, start : start + width]
        low, high = jnp.where(first, mine, other), jnp.where(first, other, mine)
        return low.astype(F32), high.astype(F32)

    def gain(slot, pair, start):
        low = both(pair, start, OUT_PAD - OUT_HALF)[0]
        gain_ref[slot] = by_columns(chooser, low.astype(BF))

    for layer, (pair, start) in enumerate(((4, 0), (6, 0))):
        for at in range(3):
            low, high = both(pair, at * hid, hid)
            outs[4 + at][:, layer, :hid] = low[:PER]
            outs[4 + at][:, layer, hid:] = high[:PER]
    for layer, (pair, start) in enumerate(((0, QKV_PAD), (2, QKV_PAD))):
        low, high = both(pair, start, OUT_HALF)
        out_ref[:, :OUT_HALF] = low
        out_ref[:, OUT_HALF:] = high
        outs[3][:, layer, :] = out_ref[:PER, :]
        gain(2 + layer, pair, start + OUT_HALF)
    for layer, pair in enumerate((0, 2)):
        low, high = both(pair, 0, QKV_HALF)
        qkv_ref[:, :QKV_HALF] = low
        qkv_ref[:, QKV_HALF:] = high
        outs[0][:, layer, :] = qkv_ref[:PER, :QW]
        outs[1][:, layer, :] = qkv_ref[:PER, QW : QW + KVW]
        outs[2][:, layer, :] = qkv_ref[:PER, QW + KVW :]
        gain(layer, pair, QKV_HALF)


def write_grads(flag, parts):
    hid = parts[4].shape[1] // 3
    shapes = [(PER, 2, width) for width in (QW, KVW, KVW, QW, 2 * hid, 2 * hid, 2 * hid)]
    outs = pl.pallas_call(
        write_kernel,
        out_shape=tuple(jax.ShapeDtypeStruct(shape, F32) for shape in shapes + [(4, 8, PAD)]),
        in_specs=[pl.BlockSpec(memory_space=pltpu.SMEM)] + [VM] * 8,
        out_specs=(VM,) * 8,
        scratch_shapes=[pltpu.VMEM((PAD, QW + 2 * KVW), F32), pltpu.VMEM((PAD, QW), F32)],
        compiler_params=pltpu.CompilerParams(vmem_limit_bytes=40 * 2**20),
        name="write_grads",
    )(flag, *parts)
    return [jnp.swapaxes(out, 0, 1) for out in outs[:7]] + [outs[7]]


def scatter_plane(total):
    return lax.psum_scatter(total, XY, scatter_dimension=0, tiled=True)


def rope_tables(positions):
    half_head = HEAD // 2
    freqs = THETA ** (-2.0 * jnp.arange(half_head, dtype=F32) / HEAD)
    angles = positions.astype(F32)[:, None] * freqs[None, :]
    return (jnp.cos(angles), jnp.sin(angles))


def rotate(values, cosine, sine, direction):
    row_count = values.shape[0]
    split_view = values.reshape(row_count, -1, 2, HEAD // 2)
    first_half = split_view[:, :, 0]
    second_half = split_view[:, :, 1]
    cos_rows = cosine[:, None, :]
    sin_rows = direction * sine[:, None, :]
    turned = jnp.stack(
        [
            first_half * cos_rows - second_half * sin_rows,
            second_half * cos_rows + first_half * sin_rows,
        ],
        axis=2,
    )
    return turned.reshape(row_count, -1)


def rms_forward(values, gain):
    mean = jnp.sum(values * values, axis=-1, keepdims=True) * (1.0 / D)
    scale = lax.rsqrt(mean + EPSILON)
    return (values * scale * gain, scale)


def rms_backward(values, scale, gain, grad_normed):
    weighted = grad_normed * gain
    mean = jnp.sum(weighted * values, axis=-1, keepdims=True) * (1.0 / D)
    grad_values = scale * weighted - values * (scale * scale * scale) * mean
    return (grad_values, (grad_normed * values * scale).astype(BF))


SHARE = HEADS // KV_HEADS


def head_stack(ref, group):
    return jnp.concatenate(
        [
            ref[:, (group * SHARE + at) * HEAD : (group * SHARE + at + 1) * HEAD]
            for at in range(SHARE)
        ],
        axis=0,
    )


def mask_bias(codes):
    segment_q, position_q, segment_k, position_k = codes
    seen = (segment_k[...] == segment_q[...]) & (position_k[...] <= position_q[...])
    return jnp.where(seen, 0.0, MASKED)


def both_rows(near, far, start):
    return jnp.concatenate(
        [near[:, start : start + HEAD], far[:, start : start + HEAD]], axis=0
    )


def attend_kernel(q_ref, near, far, sq, pq, sk, pk, att_ref, lse_ref, bias_ref):
    rows = q_ref.shape[0]
    bias_ref[...] = mask_bias((sq, pq, sk, pk))
    for group in range(KV_HEADS):
        query = head_stack(q_ref, group) * BF(HEAD ** (-0.5))
        key = both_rows(near, far, group * HEAD)
        value = both_rows(near, far, KVW + group * HEAD)
        scores = by_columns(key, query) + bias_ref[...]
        top = jnp.max(scores, axis=0, keepdims=True)
        terms = jnp.exp(scores - top)
        total = jnp.sum(terms, axis=0, keepdims=True)
        lse_ref[group : group + 1, :] = top + jnp.log(total)
        out = (by_rows(value, terms.astype(BF)) * (1.0 / total)).T
        for at in range(SHARE):
            head = group * SHARE + at
            att_ref[:, head * HEAD : (head + 1) * HEAD] = out[
                at * rows : (at + 1) * rows
            ].astype(BF)


def attend_back_kernel(
    q_ref, near, far, da_ref, lse_ref, sq, pq, sk, pk, dq_ref, near_out, far_out, bias_ref
):
    half = near.shape[0]
    rows = q_ref.shape[0]
    bias_ref[...] = mask_bias((sq, pq, sk, pk))
    for group in range(KV_HEADS):
        query = head_stack(q_ref, group) * BF(HEAD ** (-0.5))
        grad = head_stack(da_ref, group)
        key = both_rows(near, far, group * HEAD)
        value = both_rows(near, far, KVW + group * HEAD)
        probs = jnp.exp(by_columns(key, query) + bias_ref[...] - lse_ref[group : group + 1, :])
        grad_probs = by_columns(value, grad)
        delta = jnp.sum(probs * grad_probs, axis=0, keepdims=True)
        grad_scores = (probs * (grad_probs - delta)).astype(BF)
        for start, part in (
            (group * HEAD, product(grad_scores, query)),
            (KVW + group * HEAD, product(probs.astype(BF), grad)),
        ):
            near_out[:, start : start + HEAD] = part[:half]
            far_out[:, start : start + HEAD] = part[half:].astype(BF)
        out = (by_rows(key, grad_scores) * (HEAD ** (-0.5))).T
        for at in range(SHARE):
            head = group * SHARE + at
            dq_ref[:, head * HEAD : (head + 1) * HEAD] = out[at * rows : (at + 1) * rows]


def attention(query, key_value, codes):
    rows, keys = query.shape[0], 2 * key_value[0].shape[0]
    return pl.pallas_call(
        attend_kernel,
        out_shape=(
            jax.ShapeDtypeStruct((rows, QW), BF),
            jax.ShapeDtypeStruct((8, SHARE * rows), F32),
        ),
        in_specs=[VM] * 7,
        out_specs=(VM, VM),
        scratch_shapes=[pltpu.VMEM((keys, SHARE * rows), F32)],
        compiler_params=pltpu.CompilerParams(vmem_limit_bytes=40 * 2**20),
        cost_estimate=pl.CostEstimate(
            flops=16 * HEADS * HEAD * rows * keys,
            bytes_accessed=4 * 2**20,
            transcendentals=HEADS * rows * keys,
        ),
        name="attend",
    )(query, *key_value, *codes)


def attention_back(query, key_value, grad_attended_b, log_totals, codes):
    rows, keys = query.shape[0], 2 * key_value[0].shape[0]
    return pl.pallas_call(
        attend_back_kernel,
        out_shape=(
            jax.ShapeDtypeStruct((rows, QW), F32),
            jax.ShapeDtypeStruct((keys // 2, 2 * KVW), F32),
            jax.ShapeDtypeStruct((keys // 2, 2 * KVW), BF),
        ),
        in_specs=[VM] * 9,
        out_specs=(VM,) * 3,
        scratch_shapes=[pltpu.VMEM((keys, SHARE * rows), F32)],
        compiler_params=pltpu.CompilerParams(vmem_limit_bytes=48 * 2**20),
        cost_estimate=pl.CostEstimate(
            flops=40 * HEADS * HEAD * rows * keys,
            bytes_accessed=6 * 2**20,
            transcendentals=HEADS * rows * keys,
        ),
        name="attend_back",
    )(query, *key_value, grad_attended_b, log_totals, *codes)


def pad_features(values):
    rows = values.shape[0]
    view = values.reshape(rows, Y * X, PER)
    return jnp.pad(view, ((0, 0), (0, 0), (0, PAD - PER))).reshape(rows, DP)


def cut_features(values):
    rows = values.shape[0]
    return values.reshape(rows, Y * X, PAD)[:, :, :PER].reshape(rows, D)


def shards(
    tokens,
    segment_ids,
    positions,
    cotangent,
    attn_gain,
    w_query,
    w_key,
    w_value,
    w_out,
    ffn_gain,
    w_gate,
    w_up,
    w_down,
):
    layers = attn_gain.shape[0]
    rows = tokens.shape[0]
    hid = w_gate.shape[2] // 2
    first_core = lax.axis_index("core") == 0

    def pick(low, high):
        return jnp.where(first_core, low, high), jnp.where(first_core, high, low)

    def halves(whole, width):
        return pick(whole[..., :width], whole[..., width:])

    def join(mine, other):
        low, high = pick(mine, other)
        return jnp.concatenate([low, high], axis=-1)

    def tall(values):
        return jnp.pad(values, ((0, PAD - PER), (0, 0)))

    gain_columns = jnp.stack(
        [attn_gain[layer] for layer in range(layers)] + [ffn_gain[layer] for layer in range(layers)],
        axis=1,
    )
    gain_columns = jnp.pad(gain_columns, ((0, 0), (0, OUT_PAD - OUT_HALF - 2 * layers)))
    packs = []
    for layer in range(layers):
        qkv = jnp.concatenate([w_query[layer], w_key[layer], w_value[layer]], axis=1)
        qkv_mine = jnp.pad(halves(qkv, QKV_HALF)[0], ((0, 0), (0, QKV_PAD - QKV_HALF)))
        out_mine = halves(w_out[layer], OUT_HALF)[0]
        packs.append(jnp.concatenate([qkv_mine, out_mine, gain_columns], axis=1))
        packs.append(
            jnp.concatenate(
                [halves(w[layer], hid)[0] for w in (w_gate, w_up, w_down)], axis=1
            )
        )
    packs = [tall(pack) for pack in packs]
    cosine, sine = rope_tables(positions)
    stamps = jnp.concatenate(
        gather_group(jnp.stack([segment_ids, positions], axis=1)), axis=0
    )
    codes = (
        jnp.tile(segment_ids, SHARE)[None, :],
        jnp.tile(positions, SHARE)[None, :],
        stamps[:, :1],
        stamps[:, 1:],
    )
    stream = pad_features(tokens)
    grad_stream = pad_features(cotangent)
    att_mine, att_other, ffn_mine, ffn_other = [], [], [], []
    for layer in range(layers):
        whole = lax.all_gather(
            jnp.concatenate(packs[2 * layer : 2 * layer + 2], axis=1), XY, axis=0, tiled=True
        )
        if layer == 0:
            whole, stream, grad_stream, codes, cosine, sine = lax.optimization_barrier(
                (whole, stream, grad_stream, codes, cosine, sine)
            )
        att = whole[:, :ATT]
        ffn = whole[:, ATT:]
        for part, att_list, ffn_list in (
            ((att, ffn), att_mine, ffn_mine),
            ((swap(att, "core"), swap(ffn, "core")), att_other, ffn_other),
        ):
            att_list.append((part[0][:, :QKV_PAD], part[0][:, QKV_PAD:]))
            ffn_list.append((part[1][:, : 2 * hid], part[1][:, 2 * hid :]))

    chooser = jnp.eye(8, OUT_PAD - OUT_HALF, dtype=BF)
    gains = by_columns(chooser, att_mine[0][1][:, OUT_HALF:])
    gain_ones = [gains[layer : layer + 1] for layer in range(layers)]
    gain_twos = [gains[layers + layer : layers + layer + 1] for layer in range(layers)]

    saved = []
    for layer in range(layers):
        qkv_m, out_m = att_mine[layer]
        qkv_o, out_o = att_other[layer]
        gu_m, down_m = ffn_mine[layer]
        gu_o, down_o = ffn_other[layer]
        normed_one, scale_one = rms_forward(stream, gain_ones[layer])
        normed_one = normed_one.astype(BF)
        qkv = join(
            product(normed_one, qkv_m)[:, :QKV_HALF], product(normed_one, qkv_o)[:, :QKV_HALF]
        )
        turned = rotate(qkv[:, : QW + KVW], cosine, sine, 1.0).astype(BF)
        query = turned[:, :QW]
        key_value = jnp.concatenate([turned[:, QW:], qkv[:, QW + KVW :].astype(BF)], axis=1)
        key_value = gather_group(key_value)
        attended, log_totals = attention(query, key_value, codes)
        att_m, att_o = halves(attended, OUT_HALF)
        mixed = (
            stream
            + by_columns(att_m, out_m[:, :OUT_HALF])
            + by_columns(att_o, out_o[:, :OUT_HALF])
        )
        normed_two, scale_two = rms_forward(mixed, gain_twos[layer])
        normed_two = normed_two.astype(BF)
        normed_pair = jnp.concatenate([normed_two, swap(normed_two, "tp")], axis=0)
        hiddens = []
        kept = []
        for weight in (gu_m, gu_o):
            both = product(normed_pair, weight)
            gate, up_value = both[:, :hid], both[:, hid:]
            sigma = jax.nn.sigmoid(gate)
            hidden = (gate * sigma * up_value).astype(BF)
            hiddens.append(hidden)
            kept.append((gate, up_value, hidden))
        partial = by_columns(hiddens[0], down_m) + by_columns(hiddens[1], down_o)
        saved.append(
            (
                stream,
                scale_one,
                normed_one,
                query,
                key_value,
                log_totals,
                att_m,
                mixed,
                scale_two,
                normed_pair,
                kept,
                (
                    swap(normed_one, "core"),
                    swap(att_o, "core"),
                    swap(normed_pair, "core"),
                    swap(hiddens[1], "core"),
                ),
            )
        )
        stream = mixed + partial[:rows] + swap(partial[rows:].astype(BF), "tp").astype(F32)

    for layer in reversed(range(layers)):
        qkv_m, out_m = att_mine[layer]
        qkv_o, out_o = att_other[layer]
        gu_m, down_m = ffn_mine[layer]
        gu_o, down_o = ffn_other[layer]
        (
            layer_input,
            scale_one,
            normed_one,
            query,
            key_value,
            log_totals,
            att_m,
            mixed,
            scale_two,
            normed_pair,
            kept,
            (far_one, far_att, far_pair, far_hidden),
        ) = saved[layer]
        grad_out_b = grad_stream.astype(BF)
        grad_pair = jnp.concatenate([grad_out_b, swap(grad_out_b, "tp")], axis=0)
        far_grad_pair = swap(grad_pair, "core")
        partial = 0.0
        ffn_grads = []
        for (gate, up_value, hidden), gu, down in (
            (kept[0], gu_m, down_m),
            (kept[1], gu_o, down_o),
        ):
            grad_hidden = product(grad_pair, down)
            sigma = jax.nn.sigmoid(gate)
            grad_up_in = (grad_hidden * gate * sigma).astype(BF)
            grad_gate_in = (
                grad_hidden * up_value * sigma * (1.0 + gate * (1.0 - sigma))
            ).astype(BF)
            grad_gu = jnp.concatenate([grad_gate_in, grad_up_in], axis=1)
            partial = partial + by_columns(grad_gu, gu)
            ffn_grads.append(grad_gu)
        arrived = swap(partial[rows:].astype(BF), "tp")
        ffn_sections = [
            (normed_pair, ffn_grads[0], far_pair, swap(ffn_grads[1], "core")),
            (grad_pair, kept[0][2], far_grad_pair, far_hidden),
        ]
        if layer > 0:
            group_one = weight_grads(ffn_sections)
            arrived, group_one = lax.optimization_barrier((arrived, group_one))
            done_one = scatter_plane(group_one)
        else:
            group_two = weight_grads(att_sections + ffn_sections)
            arrived, group_two, done_one = lax.optimization_barrier(
                (arrived, group_two, done_one)
            )
            done_two = scatter_plane(group_two)
        grad_normed_two = partial[:rows] + arrived.astype(F32)
        grad_mixed_norm, gain_two_terms = rms_backward(
            mixed, scale_two, gain_twos[layer], grad_normed_two
        )
        grad_mixed = grad_stream + grad_mixed_norm
        grad_mixed_b = grad_mixed.astype(BF)
        grad_attended_b = join(
            product(grad_mixed_b, out_m)[:, :OUT_HALF], product(grad_mixed_b, out_o)[:, :OUT_HALF]
        ).astype(BF)
        far_mixed = swap(jnp.concatenate([grad_mixed_b, gain_two_terms], axis=0), "core")
        grad_query, near_terms, far_terms = attention_back(
            query, key_value, grad_attended_b, log_totals, codes
        )
        key_value_grad = scatter_group(near_terms, far_terms)
        grad_qkv = jnp.concatenate(
            [
                rotate(
                    jnp.concatenate([grad_query, key_value_grad[:, :KVW]], axis=1),
                    cosine,
                    sine,
                    -1.0,
                ),
                key_value_grad[:, KVW:],
            ],
            axis=1,
        ).astype(BF)
        grad_m, grad_o = halves(grad_qkv, QKV_HALF)
        wide = ((0, 0), (0, QKV_PAD - QKV_HALF))
        grad_m, grad_o = jnp.pad(grad_m, wide), jnp.pad(grad_o, wide)
        grad_normed_one = by_columns(grad_m, qkv_m) + by_columns(grad_o, qkv_o)
        grad_input_norm, gain_one_terms = rms_backward(
            layer_input, scale_one, gain_ones[layer], grad_normed_one
        )
        grad_stream = grad_mixed + grad_input_norm
        wide_ones = jnp.ones((rows, QKV_PAD - QKV_HALF), BF)
        ones = jnp.ones((rows, OUT_PAD - OUT_HALF), BF)
        far_qkv = swap(grad_o[:, :QKV_HALF], "core")
        att_sections = [
            (normed_one, grad_m[:, :QKV_HALF], far_one, far_qkv),
            (gain_one_terms, wide_ones, swap(gain_one_terms, "core"), wide_ones),
            (grad_mixed_b, att_m, far_mixed[:rows], far_att),
            (gain_two_terms, ones, far_mixed[rows:], ones),
        ]

    ffn_one = low_sum(done_one)
    total = weight_grads(att_sections)
    total, ffn_one = lax.optimization_barrier((total, ffn_one))
    total, block_out, input_grad, done_two = plane_scatter(
        total, 768, (cut_features(stream), cut_features(grad_stream), done_two)
    )
    att_one = z_sum(done_two[:, :ATT])
    ffn_zero = low_sum(done_two[:, ATT:])
    total, att_one, ffn_zero = lax.optimization_barrier((total, att_one, ffn_zero))
    att_zero = z_sum(total)
    parts = []
    for part in (att_zero, att_one, ffn_zero, ffn_one):
        parts += [part, swap(part, "core")]
    (
        query_grads,
        key_grads,
        value_grads,
        out_grads,
        gate_grads,
        up_grads,
        down_grads,
        gain_grads,
    ) = write_grads(lax.axis_index("core").astype(jnp.int32).reshape(1), parts)
    return (
        block_out,
        input_grad,
        gain_grads[:2, 0, :PER],
        query_grads,
        key_grads,
        value_grads,
        out_grads,
        gain_grads[2:, 0, :PER],
        gate_grads,
        up_grads,
        down_grads,
    )


def solution(mesh):
    fine = Mesh(mesh.devices.reshape(Y, X, ZL, CORE, TP), ("y", "x", "zl", "core", "tp"))
    every = ("y", "x", "zl", "core", "tp")
    return jax.shard_map(
        shards,
        mesh=fine,
        in_specs=(
            P(every, None),
            P(every),
            P(every),
            P(every, None),
            P(None, XY),
            P(None, XY, None),
            P(None, XY, None),
            P(None, XY, None),
            P(None, XY, None),
            P(None, XY),
            P(None, XY, "tp"),
            P(None, XY, "tp"),
            P(None, XY, "tp"),
        ),
        out_specs=(
            P(every, None),
            P(every, None),
            P(None, XY),
            P(None, XY, None),
            P(None, XY, None),
            P(None, XY, None),
            P(None, XY, None),
            P(None, XY),
            P(None, XY, "tp"),
            P(None, XY, "tp"),
            P(None, XY, "tp"),
        ),
        check_vma=False,
    )
```

```python
import jax
import jax.numpy as jnp
from jax import lax
from jax.experimental import pallas as pl
from jax.experimental.pallas import tpu as pltpu
from jax.sharding import Mesh, PartitionSpec as P

D = 960
HEADS = 15
KV_HEADS = 5
HEAD = 64
QW = HEADS * HEAD
KVW = KV_HEADS * HEAD

EPSILON = 1e-05
THETA = 100000.0
MASKED = -1e30

Y, X, ZL, CORE, TP = 4, 4, 2, 2, 2
XY = ("y", "x")
PER = D // (Y * X)
PAD = 64
DP = PAD * Y * X
QKV_HALF = (QW + 2 * KVW) // 2
QKV_PAD = 896
OUT_HALF = QW // 2
OUT_PAD = 512
ATT = QKV_PAD + OUT_PAD
BF = jnp.bfloat16
VM = pl.BlockSpec(memory_space=pltpu.VMEM)
F32 = jnp.float32


def product(left, right):
    return jnp.dot(left, right, preferred_element_type=F32)


def by_rows(left, right):
    return lax.dot_general(left, right, (((0,), (0,)), ((), ())), preferred_element_type=F32)


def by_columns(left, right):
    return lax.dot_general(left, right, (((1,), (1,)), ((), ())), preferred_element_type=F32)


def ring(size, step):
    return [(i, (i + step) % size) for i in range(size)]


def z_ring(step):
    pairs = []
    for low in range(ZL):
        for high in range(TP):
            there = (high * ZL + low + step) % (ZL * TP)
            pairs.append((low * TP + high, (there % ZL) * TP + there // ZL))
    return pairs


def swap(values, axis):
    return lax.ppermute(values, axis, [(0, 1), (1, 0)])


def z_send(values, step):
    return lax.ppermute(values, ("zl", "tp"), z_ring(step))


STEPS = (2, 1, 3)


def gather_group(values):
    mine = jnp.concatenate([values] + [z_send(values, step) for step in STEPS], axis=0)
    return mine, swap(mine, "core")


def scatter_group(mine, other):
    rows = mine.shape[0] // 4
    total = mine + swap(other, "core").astype(F32)
    out = total[:rows]
    for at, step in enumerate(STEPS):
        block = total[(at + 1) * rows : (at + 2) * rows].astype(BF)
        out = out + z_send(block, -step).astype(F32)
    return out


def line_scatter(values, axis):
    at = lax.axis_index(axis)
    out = lax.dynamic_index_in_dim(values, at, 0, False).astype(F32)
    for step in STEPS:
        block = lax.dynamic_index_in_dim(values, (at + step) % 4, 0, False)
        out = out + lax.ppermute(block, axis, ring(4, step)).astype(F32)
    return out


def plane_scatter(values, cut, others):
    view = values.reshape(Y, X, PAD, values.shape[1])
    first = line_scatter(jnp.swapaxes(view[..., :cut], 0, 1), "x").astype(BF)
    second = line_scatter(view[..., cut:], "y").astype(BF)
    first, second, others = lax.optimization_barrier((first, second, others))
    first = line_scatter(first, "y")
    second = line_scatter(second, "x")
    return (jnp.concatenate([first, second], axis=1),) + others


def low_sum(part):
    part = part.astype(BF)
    return (part.astype(F32) + swap(part, "zl").astype(F32)).astype(BF)


def z_sum(part):
    part = part.astype(BF)
    two, one, three = (z_send(part, step).astype(F32) for step in STEPS)
    return ((part.astype(F32) + two) + (one + three)).astype(BF)


def weight_grads(sections):
    operands, spans, base = [], [], 0
    for section in sections:
        width = section[1].shape[1]
        spans.append((len(operands), base, base + width))
        operands += list(section)
        base += width

    def kernel(*refs):
        for at, start, stop in spans:
            left, right, far_left, far_right = refs[at : at + 4]
            part = by_rows(left[...], right[...]) + by_rows(far_left[...], far_right[...])
            refs[-1][:, start:stop] = part.astype(BF)

    return pl.pallas_call(
        kernel,
        out_shape=jax.ShapeDtypeStruct((DP, base), BF),
        in_specs=[VM] * len(operands),
        out_specs=VM,
        compiler_params=pltpu.CompilerParams(vmem_limit_bytes=48 * 2**20),
        cost_estimate=pl.CostEstimate(
            flops=2 * DP * base * 640, bytes_accessed=4 * DP * base, transcendentals=0
        ),
        name="weight_grads",
    )(*operands)


def write_kernel(flag_ref, *refs):
    ins, outs, gain_ref, qkv_ref, out_ref = refs[:8], refs[8:15], *refs[15:]
    first = flag_ref[0] == 0
    shape = (8, OUT_PAD - OUT_HALF)
    chooser = (
        lax.broadcasted_iota(jnp.int32, shape, 0) == lax.broadcasted_iota(jnp.int32, shape, 1)
    ).astype(BF)
    hid = ins[4].shape[1] // 3

    def both(pair, start, width):
        mine, other = ins[pair][:, start : start + width], ins[pair + 1][:, start : start + width]
        low, high = jnp.where(first, mine, other), jnp.where(first, other, mine)
        return low.astype(F32), high.astype(F32)

    def gain(slot, pair, start):
        low = both(pair, start, OUT_PAD - OUT_HALF)[0]
        gain_ref[slot] = by_columns(chooser, low.astype(BF))

    for layer, (pair, start) in enumerate(((4, 0), (6, 0))):
        for at in range(3):
            low, high = both(pair, at * hid, hid)
            outs[4 + at][:, layer, :hid] = low[:PER]
            outs[4 + at][:, layer, hid:] = high[:PER]
    for layer, (pair, start) in enumerate(((0, QKV_PAD), (2, QKV_PAD))):
        low, high = both(pair, start, OUT_HALF)
        out_ref[:, :OUT_HALF] = low
        out_ref[:, OUT_HALF:] = high
        outs[3][:, layer, :] = out_ref[:PER, :]
        gain(2 + layer, pair, start + OUT_HALF)
    for layer, pair in enumerate((0, 2)):
        low, high = both(pair, 0, QKV_HALF)
        qkv_ref[:, :QKV_HALF] = low
        qkv_ref[:, QKV_HALF:] = high
        outs[0][:, layer, :] = qkv_ref[:PER, :QW]
        outs[1][:, layer, :] = qkv_ref[:PER, QW : QW + KVW]
        outs[2][:, layer, :] = qkv_ref[:PER, QW + KVW :]
        gain(layer, pair, QKV_HALF)


def write_grads(flag, parts):
    hid = parts[4].shape[1] // 3
    shapes = [(PER, 2, width) for width in (QW, KVW, KVW, QW, 2 * hid, 2 * hid, 2 * hid)]
    outs = pl.pallas_call(
        write_kernel,
        out_shape=tuple(jax.ShapeDtypeStruct(shape, F32) for shape in shapes + [(4, 8, PAD)]),
        in_specs=[pl.BlockSpec(memory_space=pltpu.SMEM)] + [VM] * 8,
        out_specs=(VM,) * 8,
        scratch_shapes=[pltpu.VMEM((PAD, QW + 2 * KVW), F32), pltpu.VMEM((PAD, QW), F32)],
        compiler_params=pltpu.CompilerParams(vmem_limit_bytes=40 * 2**20),
        name="write_grads",
    )(flag, *parts)
    return [jnp.swapaxes(out, 0, 1) for out in outs[:7]] + [outs[7]]


def scatter_plane(total):
    return lax.psum_scatter(total, XY, scatter_dimension=0, tiled=True)


def rope_tables(positions):
    half_head = HEAD // 2
    freqs = THETA ** (-2.0 * jnp.arange(half_head, dtype=F32) / HEAD)
    angles = positions.astype(F32)[:, None] * freqs[None, :]
    return (jnp.cos(angles), jnp.sin(angles))


def rotate(values, cosine, sine, direction):
    row_count = values.shape[0]
    split_view = values.reshape(row_count, -1, 2, HEAD // 2)
    first_half = split_view[:, :, 0]
    second_half = split_view[:, :, 1]
    cos_rows = cosine[:, None, :]
    sin_rows = direction * sine[:, None, :]
    turned = jnp.stack(
        [
            first_half * cos_rows - second_half * sin_rows,
            second_half * cos_rows + first_half * sin_rows,
        ],
        axis=2,
    )
    return turned.reshape(row_count, -1)


def rms_forward(values, gain):
    mean = jnp.sum(values * values, axis=-1, keepdims=True) * (1.0 / D)
    scale = lax.rsqrt(mean + EPSILON)
    return (values * scale * gain, scale)


def rms_backward(values, scale, gain, grad_normed):
    weighted = grad_normed * gain
    mean = jnp.sum(weighted * values, axis=-1, keepdims=True) * (1.0 / D)
    grad_values = scale * weighted - values * (scale * scale * scale) * mean
    return (grad_values, (grad_normed * values * scale).astype(BF))


SHARE = HEADS // KV_HEADS


def head_stack(ref, group):
    return jnp.concatenate(
        [
            ref[:, (group * SHARE + at) * HEAD : (group * SHARE + at + 1) * HEAD]
            for at in range(SHARE)
        ],
        axis=0,
    )


def mask_bias(codes):
    segment_q, position_q, segment_k, position_k = codes
    seen = (segment_k[...] == segment_q[...]) & (position_k[...] <= position_q[...])
    return jnp.where(seen, 0.0, MASKED)


def both_rows(near, far, start):
    return jnp.concatenate(
        [near[:, start : start + HEAD], far[:, start : start + HEAD]], axis=0
    )


def attend_kernel(q_ref, near, far, sq, pq, sk, pk, att_ref, lse_ref, bias_ref):
    rows = q_ref.shape[0]
    bias_ref[...] = mask_bias((sq, pq, sk, pk))
    for group in range(KV_HEADS):
        query = head_stack(q_ref, group) * BF(HEAD ** (-0.5))
        key = both_rows(near, far, group * HEAD)
        value = both_rows(near, far, KVW + group * HEAD)
        scores = by_columns(key, query) + bias_ref[...]
        top = jnp.max(scores, axis=0, keepdims=True)
        terms = jnp.exp(scores - top)
        total = jnp.sum(terms, axis=0, keepdims=True)
        lse_ref[group : group + 1, :] = top + jnp.log(total)
        out = (by_rows(value, terms.astype(BF)) * (1.0 / total)).T
        for at in range(SHARE):
            head = group * SHARE + at
            att_ref[:, head * HEAD : (head + 1) * HEAD] = out[
                at * rows : (at + 1) * rows
            ].astype(BF)


def attend_back_kernel(
    q_ref, near, far, da_ref, lse_ref, sq, pq, sk, pk, dq_ref, near_out, far_out, bias_ref
):
    half = near.shape[0]
    rows = q_ref.shape[0]
    bias_ref[...] = mask_bias((sq, pq, sk, pk))
    for group in range(KV_HEADS):
        query = head_stack(q_ref, group) * BF(HEAD ** (-0.5))
        grad = head_stack(da_ref, group)
        key = both_rows(near, far, group * HEAD)
        value = both_rows(near, far, KVW + group * HEAD)
        probs = jnp.exp(by_columns(key, query) + bias_ref[...] - lse_ref[group : group + 1, :])
        grad_probs = by_columns(value, grad)
        delta = jnp.sum(probs * grad_probs, axis=0, keepdims=True)
        grad_scores = (probs * (grad_probs - delta)).astype(BF)
        for start, part in (
            (group * HEAD, product(grad_scores, query)),
            (KVW + group * HEAD, product(probs.astype(BF), grad)),
        ):
            near_out[:, start : start + HEAD] = part[:half]
            far_out[:, start : start + HEAD] = part[half:].astype(BF)
        out = (by_rows(key, grad_scores) * (HEAD ** (-0.5))).T
        for at in range(SHARE):
            head = group * SHARE + at
            dq_ref[:, head * HEAD : (head + 1) * HEAD] = out[at * rows : (at + 1) * rows]


def attention(query, key_value, codes):
    rows, keys = query.shape[0], 2 * key_value[0].shape[0]
    return pl.pallas_call(
        attend_kernel,
        out_shape=(
            jax.ShapeDtypeStruct((rows, QW), BF),
            jax.ShapeDtypeStruct((8, SHARE * rows), F32),
        ),
        in_specs=[VM] * 7,
        out_specs=(VM, VM),
        scratch_shapes=[pltpu.VMEM((keys, SHARE * rows), F32)],
        compiler_params=pltpu.CompilerParams(vmem_limit_bytes=40 * 2**20),
        cost_estimate=pl.CostEstimate(
            flops=16 * HEADS * HEAD * rows * keys,
            bytes_accessed=4 * 2**20,
            transcendentals=HEADS * rows * keys,
        ),
        name="attend",
    )(query, *key_value, *codes)


def attention_back(query, key_value, grad_attended_b, log_totals, codes):
    rows, keys = query.shape[0], 2 * key_value[0].shape[0]
    return pl.pallas_call(
        attend_back_kernel,
        out_shape=(
            jax.ShapeDtypeStruct((rows, QW), F32),
            jax.ShapeDtypeStruct((keys // 2, 2 * KVW), F32),
            jax.ShapeDtypeStruct((keys // 2, 2 * KVW), BF),
        ),
        in_specs=[VM] * 9,
        out_specs=(VM,) * 3,
        scratch_shapes=[pltpu.VMEM((keys, SHARE * rows), F32)],
        compiler_params=pltpu.CompilerParams(vmem_limit_bytes=48 * 2**20),
        cost_estimate=pl.CostEstimate(
            flops=40 * HEADS * HEAD * rows * keys,
            bytes_accessed=6 * 2**20,
            transcendentals=HEADS * rows * keys,
        ),
        name="attend_back",
    )(query, *key_value, grad_attended_b, log_totals, *codes)


def pad_features(values):
    rows = values.shape[0]
    view = values.reshape(rows, Y * X, PER)
    return jnp.pad(view, ((0, 0), (0, 0), (0, PAD - PER))).reshape(rows, DP)


def cut_features(values):
    rows = values.shape[0]
    return values.reshape(rows, Y * X, PAD)[:, :, :PER].reshape(rows, D)


def shards(
    tokens,
    segment_ids,
    positions,
    cotangent,
    attn_gain,
    w_query,
    w_key,
    w_value,
    w_out,
    ffn_gain,
    w_gate,
    w_up,
    w_down,
):
    layers = attn_gain.shape[0]
    rows = tokens.shape[0]
    hid = w_gate.shape[2] // 2
    first_core = lax.axis_index("core") == 0

    def pick(low, high):
        return jnp.where(first_core, low, high), jnp.where(first_core, high, low)

    def halves(whole, width):
        return pick(whole[..., :width], whole[..., width:])

    def join(mine, other):
        low, high = pick(mine, other)
        return jnp.concatenate([low, high], axis=-1)

    def tall(values):
        return jnp.pad(values, ((0, PAD - PER), (0, 0)))

    gain_columns = jnp.stack(
        [attn_gain[layer] for layer in range(layers)] + [ffn_gain[layer] for layer in range(layers)],
        axis=1,
    )
    gain_columns = jnp.pad(gain_columns, ((0, 0), (0, OUT_PAD - OUT_HALF - 2 * layers)))
    packs = []
    for layer in range(layers):
        qkv = jnp.concatenate([w_query[layer], w_key[layer], w_value[layer]], axis=1)
        qkv_mine = jnp.pad(halves(qkv, QKV_HALF)[0], ((0, 0), (0, QKV_PAD - QKV_HALF)))
        out_mine = halves(w_out[layer], OUT_HALF)[0]
        packs.append(jnp.concatenate([qkv_mine, out_mine, gain_columns], axis=1))
        packs.append(
            jnp.concatenate(
                [halves(w[layer], hid)[0] for w in (w_gate, w_up, w_down)], axis=1
            )
        )
    packs = [tall(pack) for pack in packs]
    cosine, sine = rope_tables(positions)
    stamps = jnp.concatenate(
        gather_group(jnp.stack([segment_ids, positions], axis=1)), axis=0
    )
    codes = (
        jnp.tile(segment_ids, SHARE)[None, :],
        jnp.tile(positions, SHARE)[None, :],
        stamps[:, :1],
        stamps[:, 1:],
    )
    stream = pad_features(tokens)
    grad_stream = pad_features(cotangent)
    att_mine, att_other, ffn_mine, ffn_other, wholes = [], [], [], [], []
    for layer in range(layers):
        whole = lax.all_gather(
            jnp.concatenate(packs[2 * layer : 2 * layer + 2], axis=1), XY, axis=0, tiled=True
        )
        if layer == 0:
            whole, stream, grad_stream, codes, cosine, sine = lax.optimization_barrier(
                (whole, stream, grad_stream, codes, cosine, sine)
            )
        wholes.append(whole)

    def split_whole(whole):
        att = whole[:, :ATT]
        ffn = whole[:, ATT:]
        for part, att_list, ffn_list in (
            ((att, ffn), att_mine, ffn_mine),
            ((swap(att, "core"), swap(ffn, "core")), att_other, ffn_other),
        ):
            att_list.append((part[0][:, :QKV_PAD], part[0][:, QKV_PAD:]))
            ffn_list.append((part[1][:, : 2 * hid], part[1][:, 2 * hid :]))

    split_whole(wholes[0])
    chooser = jnp.eye(8, OUT_PAD - OUT_HALF, dtype=BF)
    gains = by_columns(chooser, att_mine[0][1][:, OUT_HALF:])
    gain_ones = [gains[layer : layer + 1] for layer in range(layers)]
    gain_twos = [gains[layers + layer : layers + layer + 1] for layer in range(layers)]

    saved = []
    for layer in range(layers):
        qkv_m, out_m = att_mine[layer]
        qkv_o, out_o = att_other[layer]
        gu_m, down_m = ffn_mine[layer]
        gu_o, down_o = ffn_other[layer]
        normed_one, scale_one = rms_forward(stream, gain_ones[layer])
        normed_one = normed_one.astype(BF)
        qkv = join(
            product(normed_one, qkv_m)[:, :QKV_HALF], product(normed_one, qkv_o)[:, :QKV_HALF]
        )
        turned = rotate(qkv[:, : QW + KVW], cosine, sine, 1.0).astype(BF)
        query = turned[:, :QW]
        key_value = jnp.concatenate([turned[:, QW:], qkv[:, QW + KVW :].astype(BF)], axis=1)
        key_value = gather_group(key_value)
        attended, log_totals = attention(query, key_value, codes)
        att_m, att_o = halves(attended, OUT_HALF)
        mixed = (
            stream
            + by_columns(att_m, out_m[:, :OUT_HALF])
            + by_columns(att_o, out_o[:, :OUT_HALF])
        )
        normed_two, scale_two = rms_forward(mixed, gain_twos[layer])
        normed_two = normed_two.astype(BF)
        normed_pair = jnp.concatenate([normed_two, swap(normed_two, "tp")], axis=0)
        hiddens = []
        kept = []
        for weight in (gu_m, gu_o):
            both = product(normed_pair, weight)
            gate, up_value = both[:, :hid], both[:, hid:]
            sigma = jax.nn.sigmoid(gate)
            hidden = (gate * sigma * up_value).astype(BF)
            hiddens.append(hidden)
            kept.append((gate, up_value, hidden))
        partial = by_columns(hiddens[0], down_m) + by_columns(hiddens[1], down_o)
        if layer + 1 < layers:
            partial, later_whole = lax.optimization_barrier((partial, wholes[layer + 1]))
            split_whole(later_whole)
        saved.append(
            (
                stream,
                scale_one,
                normed_one,
                query,
                key_value,
                log_totals,
                att_m,
                mixed,
                scale_two,
                normed_pair,
                kept,
                (
                    swap(normed_one, "core"),
                    swap(att_o, "core"),
                    swap(normed_pair, "core"),
                    swap(hiddens[1], "core"),
                ),
            )
        )
        stream = mixed + partial[:rows] + swap(partial[rows:].astype(BF), "tp").astype(F32)

    for layer in reversed(range(layers)):
        qkv_m, out_m = att_mine[layer]
        qkv_o, out_o = att_other[layer]
        gu_m, down_m = ffn_mine[layer]
        gu_o, down_o = ffn_other[layer]
        (
            layer_input,
            scale_one,
            normed_one,
            query,
            key_value,
            log_totals,
            att_m,
            mixed,
            scale_two,
            normed_pair,
            kept,
            (far_one, far_att, far_pair, far_hidden),
        ) = saved[layer]
        grad_out_b = grad_stream.astype(BF)
        grad_pair = jnp.concatenate([grad_out_b, swap(grad_out_b, "tp")], axis=0)
        far_grad_pair = swap(grad_pair, "core")
        partial = 0.0
        ffn_grads = []
        for (gate, up_value, hidden), gu, down in (
            (kept[0], gu_m, down_m),
            (kept[1], gu_o, down_o),
        ):
            grad_hidden = product(grad_pair, down)
            sigma = jax.nn.sigmoid(gate)
            grad_up_in = (grad_hidden * gate * sigma).astype(BF)
            grad_gate_in = (
                grad_hidden * up_value * sigma * (1.0 + gate * (1.0 - sigma))
            ).astype(BF)
            grad_gu = jnp.concatenate([grad_gate_in, grad_up_in], axis=1)
            partial = partial + by_columns(grad_gu, gu)
            ffn_grads.append(grad_gu)
        arrived = swap(partial[rows:].astype(BF), "tp")
        ffn_sections = [
            (normed_pair, ffn_grads[0], far_pair, swap(ffn_grads[1], "core")),
            (grad_pair, kept[0][2], far_grad_pair, far_hidden),
        ]
        if layer > 0:
            group_one = weight_grads(ffn_sections)
            arrived, group_one = lax.optimization_barrier((arrived, group_one))
            done_one = scatter_plane(group_one)
        else:
            group_two = weight_grads(att_sections + ffn_sections)
            arrived, group_two, done_one = lax.optimization_barrier(
                (arrived, group_two, done_one)
            )
            done_two = scatter_plane(group_two)
        grad_normed_two = partial[:rows] + arrived.astype(F32)
        grad_mixed_norm, gain_two_terms = rms_backward(
            mixed, scale_two, gain_twos[layer], grad_normed_two
        )
        grad_mixed = grad_stream + grad_mixed_norm
        grad_mixed_b = grad_mixed.astype(BF)
        grad_attended_b = join(
            product(grad_mixed_b, out_m)[:, :OUT_HALF], product(grad_mixed_b, out_o)[:, :OUT_HALF]
        ).astype(BF)
        far_mixed = swap(jnp.concatenate([grad_mixed_b, gain_two_terms], axis=0), "core")
        grad_query, near_terms, far_terms = attention_back(
            query, key_value, grad_attended_b, log_totals, codes
        )
        key_value_grad = scatter_group(near_terms, far_terms)
        grad_qkv = jnp.concatenate(
            [
                rotate(
                    jnp.concatenate([grad_query, key_value_grad[:, :KVW]], axis=1),
                    cosine,
                    sine,
                    -1.0,
                ),
                key_value_grad[:, KVW:],
            ],
            axis=1,
        ).astype(BF)
        grad_m, grad_o = halves(grad_qkv, QKV_HALF)
        wide = ((0, 0), (0, QKV_PAD - QKV_HALF))
        grad_m, grad_o = jnp.pad(grad_m, wide), jnp.pad(grad_o, wide)
        grad_normed_one = by_columns(grad_m, qkv_m) + by_columns(grad_o, qkv_o)
        grad_input_norm, gain_one_terms = rms_backward(
            layer_input, scale_one, gain_ones[layer], grad_normed_one
        )
        grad_stream = grad_mixed + grad_input_norm
        wide_ones = jnp.ones((rows, QKV_PAD - QKV_HALF), BF)
        ones = jnp.ones((rows, OUT_PAD - OUT_HALF), BF)
        far_qkv = swap(grad_o[:, :QKV_HALF], "core")
        att_sections = [
            (normed_one, grad_m[:, :QKV_HALF], far_one, far_qkv),
            (gain_one_terms, wide_ones, swap(gain_one_terms, "core"), wide_ones),
            (grad_mixed_b, att_m, far_mixed[:rows], far_att),
            (gain_two_terms, ones, far_mixed[rows:], ones),
        ]

    ffn_one = low_sum(done_one)
    total = weight_grads(att_sections)
    total, ffn_one = lax.optimization_barrier((total, ffn_one))
    total, block_out, input_grad, done_two = plane_scatter(
        total, 768, (cut_features(stream), cut_features(grad_stream), done_two)
    )
    att_one = z_sum(done_two[:, :ATT])
    ffn_zero = low_sum(done_two[:, ATT:])
    total, att_one, ffn_zero = lax.optimization_barrier((total, att_one, ffn_zero))
    att_zero = z_sum(total)
    parts = []
    for part in (att_zero, att_one, ffn_zero, ffn_one):
        parts += [part, swap(part, "core")]
    (
        query_grads,
        key_grads,
        value_grads,
        out_grads,
        gate_grads,
        up_grads,
        down_grads,
        gain_grads,
    ) = write_grads(lax.axis_index("core").astype(jnp.int32).reshape(1), parts)
    return (
        block_out,
        input_grad,
        gain_grads[:2, 0, :PER],
        query_grads,
        key_grads,
        value_grads,
        out_grads,
        gain_grads[2:, 0, :PER],
        gate_grads,
        up_grads,
        down_grads,
    )


def solution(mesh):
    fine = Mesh(mesh.devices.reshape(Y, X, ZL, CORE, TP), ("y", "x", "zl", "core", "tp"))
    every = ("y", "x", "zl", "core", "tp")
    return jax.shard_map(
        shards,
        mesh=fine,
        in_specs=(
            P(every, None),
            P(every),
            P(every),
            P(every, None),
            P(None, XY),
            P(None, XY, None),
            P(None, XY, None),
            P(None, XY, None),
            P(None, XY, None),
            P(None, XY),
            P(None, XY, "tp"),
            P(None, XY, "tp"),
            P(None, XY, "tp"),
        ),
        out_specs=(
            P(every, None),
            P(every, None),
            P(None, XY),
            P(None, XY, None),
            P(None, XY, None),
            P(None, XY, None),
            P(None, XY, None),
            P(None, XY),
            P(None, XY, "tp"),
            P(None, XY, "tp"),
            P(None, XY, "tp"),
        ),
        check_vma=False,
    )
```
